256 devices in a mesh: ctx: 64 (over x, y_lo, z), head: 4 (over y_hi, core).
Axes of the slice: x: 4, y: 4 (y_hi: 2, y_lo: 2; y = y_hi * 2 + y_lo), z: 8, core: 2. Of those that a mesh axis runs over, the one named last changes fastest.
Arguments:
- query: bfloat16 [16384, 2048], P('ctx', 'head'), may hold values from -8 to 8
- keys: bfloat16 [16384, 512], P('ctx', 'head'), may hold values from -6 to 6
- values: bfloat16 [16384, 512], P('ctx', 'head'), may hold values from -6 to 6
- out_weight: bfloat16 [2048, 4096], P('head'), may hold values from -0.125 to 0.125
Outputs:
- projected: bfloat16 [16384, 4096], P('ctx', 'head')
The draws below stay inside these ranges and needn't reach their ends.
All inputs are finite; a program needn't handle non-finite values.
Results may differ from the reference program's by a relative error of at most 0.015.
Values may be sent and summed in bfloat16 or wider, within the bound.
A program may use at most 192 MiB of HBM per device.

```python
import math
import jax
import jax.numpy as jnp
from jax import lax

D = 4096
HD = 128
QHEADS = 16
KVHEADS = 4
TOKENS = 16384


def draw_keys(key, part):
    key = jax.random.fold_in(key, 11)
    base = jnp.clip(jax.random.normal(key, (TOKENS, KVHEADS * HD), jnp.float32), -6.0, 6.0)
    return base.astype(jnp.bfloat16)


def draw_query(key, part):
    key = jax.random.fold_in(key, 23)
    base = jnp.clip(jax.random.normal(key, (TOKENS, QHEADS * HD), jnp.float32), -6.0, 6.0)
    return base.astype(jnp.bfloat16)


def block_scale(rng, shape, cuts, smallest, top_value):
    def one(dim, parts):
        draws = jax.random.uniform(jax.random.fold_in(jax.random.fold_in(rng, 6), dim), (parts,), jnp.float32, smallest / len(cuts), top_value / len(cuts))
        return jnp.repeat(jnp.exp(draws), shape[dim] // parts).reshape((-1,) + (1,) * (len(shape) - dim - 1))

    factor_of = one(*cuts[0])
    for cut in cuts[1:]:
        factor_of = factor_of * one(*cut)
    return factor_of


def bell_draw(key, shape, scale, bound, cuts=(), kind=jnp.bfloat16):
    factor_of = block_scale(key, shape, cuts, -0.22, 0.18) if cuts else 1.0
    values = jax.random.normal(key, shape, jnp.float32) * scale * factor_of
    return jnp.minimum(jnp.maximum(values, -bound), bound).astype(kind)


def setup_inputs(seed: int = 0) -> dict:
    streams_of = jax.random.split(jax.random.key(seed), 5)
    query = draw_query(jax.random.fold_in(streams_of[4], 71), 0)
    keys = draw_keys(jax.random.fold_in(streams_of[4], 71), 0)
    values = bell_draw(streams_of[2], (TOKENS, KVHEADS * HD), 1.0, 6.0, ((0, 64), (1, 4)))
    out_weight = bell_draw(streams_of[3], (QHEADS * HD, D), (QHEADS * HD) ** -0.5, 0.125, ((0, 4),))
    return {"query": query, "keys": keys, "values": values, "out_weight": out_weight}


def reference(query, keys, values, out_weight):
    group = QHEADS // KVHEADS
    block_rows = min(512, TOKENS)
    scale = 1.0 / math.sqrt(HD)
    pieces = []
    for block in range(TOKENS // block_rows):
        first = block * block_rows
        last = first + block_rows
        q_block = query[first:last].reshape(block_rows, KVHEADS, group, HD).astype(jnp.float32)
        k_block = keys[:last].reshape(last, KVHEADS, HD).astype(jnp.float32)
        v_block = values[:last].reshape(last, KVHEADS, HD).astype(jnp.float32)
        scores = jnp.einsum('tkgd,skd->kgts', q_block, k_block) * scale
        q_pos = first + jnp.arange(block_rows, dtype=jnp.int32)
        k_pos = jnp.arange(last, dtype=jnp.int32)
        allowed = k_pos[None, :] <= q_pos[:, None]
        rowmax = lax.optimization_barrier(jnp.max(jnp.where(allowed, scores, -1e+30), axis=-1))
        weights = jnp.where(allowed, jnp.exp(scores - rowmax[..., None]), 0.0)
        total = lax.optimization_barrier(jnp.sum(weights, axis=-1))
        rounded = weights.astype(jnp.bfloat16).astype(jnp.float32)
        mixed = jnp.einsum('kgts,skd->kgtd', rounded, v_block) / total[..., None]
        mixed = jnp.transpose(mixed, (2, 0, 1, 3)).reshape(block_rows, QHEADS * HD)
        pieces.append(mixed.astype(jnp.bfloat16))
    attended = jnp.concatenate(pieces, axis=0)
    return jnp.dot(attended, out_weight, preferred_element_type=jnp.float32).astype(jnp.bfloat16)
```

```python
import functools
import math

import jax
import jax.numpy as jnp
from jax import lax
from jax.experimental import pallas as pl
from jax.experimental.pallas import tpu as pltpu
from jax.sharding import PartitionSpec as P

HD = 128
ROWS = 256
NX, NZ = 4, 8
NU = 2 * NX
LOG2E = math.log2(math.e)
FLOOR = -1e30
PEN = 1e32
WCH = 4
MESH = pl.DeviceIdType.MESH
BF = jnp.bfloat16
F32 = jnp.float32


def dev(x, yl, z, yh, c):
    return {"ctx": (x * 2 + yl) * NZ + z, "head": yh * 2 + c}


def kernel(
    q_ref, k_ref, v_ref, w_ref, o_ref,
    vst, kvbuf, qbuf, s_ref, mx_ref, acc, m_ref, l_ref,
    osend, ssend, orecv, srecv, attsend, att, wbuf,
    sw_s, sw_r, qs_s, qs_r, z_s, z_r, sib_s, sib_r,
    w1_s, w1_r, w2_s, w2_r, w3_s, w3_r, wl,
    os_s, os_r, at_s, at_r, as_s, as_r,
):
    ctx = lax.axis_index("ctx")
    head = lax.axis_index("head")
    x = ctx // (2 * NZ)
    yl = (ctx // NZ) % 2
    z = ctx % NZ
    yh = head // 2
    c = head % 2
    scale = LOG2E / math.sqrt(HD)
    D = functools.partial(dev)
    zp, zm = (z + 1) % NZ, (z + NZ - 1) % NZ

    barrier = pltpu.get_barrier_semaphore()
    partners = []
    for i in range(1, 8):
        a, b, d = i // 4, (i // 2) % 2, i % 2
        partners.append(D(x, (yl + b) % 2, z, (yh + a) % 2, (c + d) % 2))
    for i in range(1, NX):
        partners.append(D((x + i) % NX, yl, z, yh, c))
    partners += [D(x, yl, zp, yh, c), D(x, yl, zm, yh, c)]
    for p in partners:
        pl.semaphore_signal(barrier, inc=1, device_id=p, device_id_type=MESH)
    vst[0:HD, :] = v_ref[0:HD, :].T
    vst[HD:ROWS, :] = v_ref[HD:ROWS, :].T
    pl.semaphore_wait(barrier, len(partners))

    def rcopy(src, dst, ss, rs, to):
        return pltpu.make_async_remote_copy(
            src_ref=src, dst_ref=dst, send_sem=ss, recv_sem=rs, device_id=to, device_id_type=MESH
        )

    sib = D(x, yl, z, yh, 1 - c)
    lo, hi = 2 * x, 2 * x + 1

    swap_to = D(x, c, z, yh, yl)
    away = c != yl

    def kv_half(slot, zz, half):
        return kvbuf.at[slot, zz, pl.ds(half * ROWS, ROWS), :]

    def q_to(d):
        return D(x, c, z, yh, d)

    def q_src(d):
        return q_ref.at[:, pl.ds(d * 2 * HD, 2 * HD)]

    kcp = rcopy(k_ref, kv_half(yl, z, 0), sw_s.at[0], sw_r.at[0], swap_to)
    vcp = rcopy(vst, kv_half(yl, z, 1), sw_s.at[1], sw_r.at[1], swap_to)
    klc = pltpu.make_async_copy(k_ref, kv_half(yl, z, 0), sw_r.at[0])
    vlc = pltpu.make_async_copy(vst, kv_half(yl, z, 1), sw_r.at[1])

    def q_remote(d):
        return rcopy(q_src(d), qbuf.at[2 * x + yl], sw_s.at[2 + d], qs_r.at[2 * x + yl], q_to(d))

    def q_local(d):
        return pltpu.make_async_copy(q_src(d), qbuf.at[2 * x + yl], qs_r.at[2 * x + yl])

    @pl.when(away)
    def _():
        kcp.start()
        vcp.start()
        for d in range(2):
            q_remote(d).start()

    @pl.when(jnp.logical_not(away))
    def _():
        klc.start()
        vlc.start()
        for d in range(2):
            @pl.when(c == d)
            def _():
                q_local(d).start()

            @pl.when(c != d)
            def _():
                q_remote(d).start()

    DC = o_ref.shape[1]
    WR = w_ref.shape[0]
    WP = WR // WCH
    gw = yh * 2 + c
    xrow = (1 - yh) * 2 + yl
    yrow = (1 - yh) * 2 + (1 - yl)

    def w1(j, d):
        return rcopy(
            w_ref.at[pl.ds(j * WP, WP), pl.ds(((1 - yh) * 2 + d) * DC, DC)],
            wbuf.at[gw, pl.ds(j * WP, WP), :],
            w1_s.at[j, d], w1_r.at[j], D(x, 1 - yl, z, 1 - yh, d),
        )

    def w1_in(j):
        return rcopy(
            wbuf.at[xrow, pl.ds(j * WP, WP), :], wbuf.at[xrow, pl.ds(j * WP, WP), :],
            w2_s.at[j], w1_r.at[j], D(x, 1 - yl, z, yh, c),
        )

    def w2(j):
        return rcopy(
            wbuf.at[xrow, pl.ds(j * WP, WP), :], wbuf.at[xrow, pl.ds(j * WP, WP), :],
            w2_s.at[j], w2_r.at[j], D(x, 1 - yl, z, yh, c),
        )

    w3 = rcopy(
        w_ref.at[:, pl.ds((yh * 2 + 1 - c) * DC, DC)], wbuf.at[gw], w3_s, w3_r, sib
    )
    wown = pltpu.make_async_copy(w_ref.at[:, pl.ds(gw * DC, DC)], wbuf.at[gw], wl)

    def blk(slot, zz):
        return kvbuf.at[slot, zz]

    def zfwd(zz, d, n, to):
        return rcopy(blk(c, zz), blk(c, zz), z_s.at[d, n], z_r.at[d, n], to)

    zup, zdn = D(x, yl, zp, yh, c), D(x, yl, zm, yh, c)
    rel = [z, zm, zp, (z + NZ - 2) % NZ, (z + 2) % NZ, (z + NZ - 3) % NZ, (z + 3) % NZ,
           (z + NZ - 4) % NZ]

    def up(n, r):
        return zfwd(rel[r], 0, n, zup)

    def down(n, r):
        return zfwd(rel[r], 1, n, zdn)

    def tosib(r):
        return rcopy(blk(c, rel[r]), blk(c, rel[r]), sib_s.at[r], sib_r.at[r], sib)

    def arrive(r):
        k = (r + 1) // 2
        if r % 2 == 1:
            zfwd(rel[r], 0, k - 1, zup).wait_recv()
        else:
            zfwd(rel[r], 1, k - 1, zdn).wait_recv()
        if r % 2 == 1 and k < 4:
            up(k, r).start()
        if r % 2 == 0 and k < 3:
            down(k, r).start()
        tosib(r).start()

    def sib_arrive(r):
        rcopy(blk(1 - c, rel[r]), blk(1 - c, rel[r]), sib_s.at[r], sib_r.at[r], sib).wait_recv()

    m_ref[...] = jnp.full_like(m_ref, FLOOR)
    l_ref[...] = jnp.zeros_like(l_ref)
    acc[...] = jnp.zeros_like(acc)

    for half in range(2):
        pltpu.make_async_copy(kv_half(c, z, half), kv_half(c, z, half), sw_r.at[half]).wait()
    up(0, 0).start()
    down(0, 0).start()
    tosib(0).start()

    @pl.when(c != yl)
    def _():
        for j in range(WCH):
            for d in range(2):
                w1(j, d).start()

    def q_wait(u):
        pltpu.make_async_copy(qbuf.at[u], qbuf.at[u], qs_r.at[u]).wait()

    q_wait(lo)
    q_wait(hi)

    def q_send(xt, s):
        u = 2 * x + s
        return rcopy(qbuf.at[u], qbuf.at[u], qs_s.at[xt, s], qs_r.at[u], D(xt, yl, z, yh, c))

    for xt in range(NX - 1):
        @pl.when(xt < x)
        def _():
            for s in range(2):
                q_send(xt, s).start()
    w3.start()
    wown.start()

    def hs(h):
        return slice(h * ROWS, (h + 1) * ROWS)

    def qk(slot, zz, u, h):
        return lax.dot_general(
            kvbuf[slot, zz, 0:ROWS, :], qbuf[u, :, h * HD:(h + 1) * HD],
            (((1,), (1,)), ((), ())), preferred_element_type=F32,
        )

    def vt(slot, zz):
        return jnp.concatenate(
            [kvbuf[slot, zz, ROWS:ROWS + HD, :], kvbuf[slot, zz, ROWS + HD:2 * ROWS, :]], axis=1
        )

    def pv(slot, zz, p):
        return lax.dot_general(
            vt(slot, zz), p.astype(BF), (((1,), (0,)), ((), ())), preferred_element_type=F32
        )

    def fold(a, op):
        return op(a.reshape(a.shape[0] // 8, 8, a.shape[1]), axis=0)

    def diagonal(slot, u):
        key_i = lax.broadcasted_iota(jnp.int32, (ROWS, ROWS), 0)
        qry_i = lax.broadcasted_iota(jnp.int32, (ROWS, ROWS), 1)
        allowed = key_i <= qry_i
        for h in range(2):
            s = jnp.where(allowed, qk(slot, z, u, h) * scale, -PEN)
            m = jnp.max(s, axis=0, keepdims=True)
            p = jnp.exp2(s - m)
            m_ref[u, 0:1, hs(h)] = m
            l_ref[u, :, hs(h)] = fold(p, jnp.sum)
            acc[u, :, hs(h)] = pv(slot, z, p)

    def pen(slot, zz, u):
        kid = (2 * x + slot) * NZ + zz
        return jnp.where(kid < u * NZ + z, 0.0, PEN).astype(F32)

    def score(slot, zs, u, h):
        mx = None
        for b in range(4):
            s = qk(slot, zs[b], u, h)
            s_ref[b * ROWS:(b + 1) * ROWS, hs(h)] = s
            top = fold(s, jnp.max) - pen(slot, zs[b], u)
            mx = top if mx is None else jnp.maximum(mx, top)
        mx_ref[:, hs(h)] = mx

    def absorb(slot, zs, u, un, h):
        m_old = m_ref[u, 0:1, hs(h)]
        m_new = jnp.maximum(m_old, jnp.max(mx_ref[:, hs(h)], axis=0, keepdims=True) * scale)
        alpha = jnp.exp2(m_old - m_new)
        m_ref[u, 0:1, hs(h)] = m_new
        l8, out = None, None
        for b in range(4):
            p = jnp.exp2(s_ref[b * ROWS:(b + 1) * ROWS, hs(h)] * scale - (m_new + pen(slot, zs[b], u)))
            p8 = fold(p, jnp.sum)
            l8 = p8 if l8 is None else l8 + p8
            d = pv(slot, zs[b], p)
            out = d if out is None else out + d
        score(slot, zs, un, h)
        l_ref[u, :, hs(h)] = l_ref[u, :, hs(h)] * alpha + l8
        acc[u, :, hs(h)] = acc[u, :, hs(h)] * alpha + out

    diagonal(c, 2 * x + c)
    arrive(1)
    arrive(2)
    sib_arrive(0)
    diagonal(1 - c, 2 * x + 1 - c)
    arrive(3)

    def o_send(u):
        return rcopy(osend.at[u], orecv.at[x, u % 2], os_s.at[u, 0], os_r.at[x, u % 2, 0],
                     D(u // 2, yl, z, yh, c))

    def st_send(u):
        return rcopy(ssend.at[u], srecv.at[x, u % 2], os_s.at[u, 1], os_r.at[x, u % 2, 1],
                     D(u // 2, yl, z, yh, c))

    def events(seg):
        if seg == 0:
            sib_arrive(1)
            sib_arrive(2)
            sib_arrive(3)
        if seg == 1:
            arrive(4)
        if seg == 3:
            arrive(5)
            arrive(6)
            w1_in(0).wait_recv()
            w2(0).start()
        if seg == 4:
            arrive(7)
            sib_arrive(4)
            sib_arrive(5)
            sib_arrive(6)
            sib_arrive(7)
        if seg in (5, 6, 7):
            w1_in(seg - 4).wait_recv()
            w2(seg - 4).start()

    def zsel(g):
        return [jnp.where(g == 0, rel[b], rel[b + 4]) for b in range(4)]

    def segment(seg, _):
        for e in range(8):
            if e != 2:
                pl.when(seg == e)(functools.partial(events, e))
        pss = seg // 2
        half = seg % 2
        slot = 1 - pss % 2
        zs = zsel(pss // 2)
        u0 = 2 * x + slot
        n = NU - u0
        mid = (n + 1) // 2
        last = pss == 3

        def at(i):
            return jnp.where(last, NU - 1 - i, u0 + i)

        @pl.when(half == 0)
        def _():
            for h in range(2):
                score(slot, zs, at(0), h)

        def one(i, _):
            u = at(i)
            un = at(jnp.minimum(i + 1, n - 1))

            @pl.when(jnp.logical_and(pss == 0, jnp.logical_and(un > u, un > hi)))
            def _():
                q_wait(un)

            for h in range(2):
                absorb(slot, zs, u, un, h)

            @pl.when(jnp.logical_and(last, u > hi))
            def _():
                osend[u] = acc[u].astype(BF)
                lsum = jnp.sum(l_ref[u], axis=0, keepdims=True)
                ssend[u] = jnp.concatenate(
                    [jnp.broadcast_to(m_ref[u, 0:1, :], (4, 2 * ROWS)),
                     jnp.broadcast_to(lsum, (4, 2 * ROWS))], axis=0)
                o_send(u).start()
                st_send(u).start()

            return 0

        lax.fori_loop(jnp.where(half == 0, 0, mid), jnp.where(half == 0, mid, n), one, 0)
        return 0

    lax.fori_loop(0, 8, segment, 0)

    for s in range(2):
        l_ref[2 * x + s] = jnp.broadcast_to(
            jnp.sum(l_ref[2 * x + s], axis=0, keepdims=True), (8, 2 * ROWS))

    def merge(xs, _):
        for s in range(2):
            u = 2 * x + s
            rcopy(osend.at[u], orecv.at[xs, s], os_s.at[u, 0], os_r.at[xs, s, 0], sib).wait_recv()
            rcopy(ssend.at[u], srecv.at[xs, s], os_s.at[u, 1], os_r.at[xs, s, 1], sib).wait_recv()
            m_old = m_ref[u, 0:1, :]
            m_in = srecv[xs, s, 0:1, :]
            m_new = jnp.maximum(m_old, m_in)
            a_old = jnp.exp2(m_old - m_new)
            a_in = jnp.exp2(m_in - m_new)
            m_ref[u, 0:1, :] = m_new
            l_ref[u, 0:1, :] = l_ref[u, 0:1, :] * a_old + srecv[xs, s, 4:5, :] * a_in
            acc[u] = acc[u] * a_old + orecv[xs, s].astype(F32) * a_in
        return 0

    lax.fori_loop(0, x, merge, 0)

    g = yh * 2 + yl

    def a_remote(s, t):
        return rcopy(attsend.at[s], att.at[g, c], at_s.at[s, t], at_r.at[g], D(x, s, z, t, c))

    def a_local(s):
        return pltpu.make_async_copy(attsend.at[s], att.at[g, c], at_r.at[g])

    for s in range(2):
        u = 2 * x + s
        for h in range(2):
            o = acc[u, :, hs(h)] / l_ref[u, 0:1, hs(h)]
            attsend[s, :, h * HD:(h + 1) * HD] = o.T.astype(BF)
        for t in range(2):
            here = jnp.logical_and(s == yl, t == yh)

            @pl.when(here)
            def _():
                a_local(s).start()

            @pl.when(jnp.logical_not(here))
            def _():
                a_remote(s, t).start()

    def a_sib(gg):
        return rcopy(att.at[gg, c], att.at[gg, c], as_s.at[gg], as_r.at[gg], sib)

    for gg in range(4):
        pltpu.make_async_copy(attsend.at[0], att.at[gg, c], at_r.at[gg]).wait()
        a_sib(gg).start()
    w3.wait_recv()
    wown.wait()
    for j in range(WCH):
        rcopy(wbuf.at[yrow, pl.ds(j * WP, WP), :], wbuf.at[yrow, pl.ds(j * WP, WP), :],
              w2_s.at[j], w2_r.at[j], sib).wait_recv()
    for gg in range(4):
        rcopy(att.at[gg, 1 - c], att.at[gg, 1 - c], as_s.at[gg], as_r.at[gg], sib).wait_recv()

    rows = jnp.concatenate([att[i // 2, i % 2] for i in range(8)], axis=1)
    for j in range(DC // 256):
        cs = slice(j * 256, (j + 1) * 256)
        wcol = jnp.concatenate([wbuf[i, :, cs] for i in range(4)], axis=0)
        o_ref[:, cs] = jnp.dot(rows, wcol, preferred_element_type=F32).astype(BF)

    @pl.when(away)
    def _():
        kcp.wait_send()
        vcp.wait_send()
        for d in range(2):
            q_remote(d).wait_send()

    @pl.when(jnp.logical_not(away))
    def _():
        for d in range(2):
            @pl.when(c != d)
            def _():
                q_remote(d).wait_send()

    @pl.when(c != yl)
    def _():
        for j in range(WCH):
            for d in range(2):
                w1(j, d).wait_send()
    for j in range(WCH):
        w2(j).wait_send()
    w3.wait_send()
    for n, r in ((0, 0), (1, 1), (2, 3), (3, 5)):
        up(n, r).wait_send()
    for n, r in ((0, 0), (1, 2), (2, 4)):
        down(n, r).wait_send()
    for r in range(8):
        tosib(r).wait_send()
    for xt in range(NX - 1):
        @pl.when(xt < x)
        def _():
            for s in range(2):
                q_send(xt, s).wait_send()

    def sent(u, _):
        o_send(u).wait_send()
        st_send(u).wait_send()
        return 0

    lax.fori_loop(2 * x + 2, NU, sent, 0)
    for s in range(2):
        for t in range(2):
            @pl.when(jnp.logical_not(jnp.logical_and(s == yl, t == yh)))
            def _():
                a_remote(s, t).wait_send()
    for gg in range(4):
        a_sib(gg).wait_send()


def per_device(query, keys, values, out_weight):
    rows = query.shape[0]
    d_model = out_weight.shape[1]
    dma = pltpu.SemaphoreType.DMA
    vm = pl.BlockSpec(memory_space=pltpu.VMEM)
    R2 = 2 * ROWS
    return pl.pallas_call(
        kernel,
        out_shape=jax.ShapeDtypeStruct((rows, d_model // 4), BF),
        in_specs=[vm, vm, vm, pl.BlockSpec(memory_space=pl.ANY)],
        out_specs=vm,
        scratch_shapes=[
            pltpu.VMEM((ROWS, HD), BF),
            pltpu.VMEM((2, NZ, R2, HD), BF),
            pltpu.VMEM((NU, ROWS, 2 * HD), BF),
            pltpu.VMEM((4 * ROWS, R2), F32),
            pltpu.VMEM((8, R2), F32),
            pltpu.VMEM((NU, HD, R2), F32),
            pltpu.VMEM((NU, 8, R2), F32),
            pltpu.VMEM((NU, 8, R2), F32),
            pltpu.VMEM((NU, HD, R2), BF),
            pltpu.VMEM((NU, 8, R2), F32),
            pltpu.VMEM((NX, 2, HD, R2), BF),
            pltpu.VMEM((NX, 2, 8, R2), F32),
            pltpu.VMEM((2, ROWS, 2 * HD), BF),
            pltpu.VMEM((4, 2, ROWS, 2 * HD), BF),
            pltpu.VMEM((4, out_weight.shape[0], d_model // 4), BF),
            dma((4,)), dma((2,)),
            dma((NX, 2)), dma((NU,)),
            dma((2, 4)), dma((2, 4)),
            dma((8,)), dma((8,)),
            dma((WCH, 2)), dma((WCH,)), dma((WCH,)), dma((WCH,)), dma, dma, dma,
            dma((NU, 2)), dma((NX, 2, 2)),
            dma((2, 2)), dma((4,)), dma((4,)), dma((4,)),
        ],
        compiler_params=pltpu.CompilerParams(
            collective_id=0, has_side_effects=True, vmem_limit_bytes=48 * 1024 * 1024
        ),
    )(query, keys, values, out_weight)


def solution(mesh):
    return jax.shard_map(
        per_device,
        mesh=mesh,
        in_specs=(P("ctx", "head"), P("ctx", "head"), P("ctx", "head"), P("head", None)),
        out_specs=P("ctx", "head"),
        check_vma=False,
    )
```

```python
import functools
import math

import jax
import jax.numpy as jnp
from jax import lax
from jax.experimental import pallas as pl
from jax.experimental.pallas import tpu as pltpu
from jax.sharding import PartitionSpec as P

HD = 128
ROWS = 256
NX, NZ = 4, 8
NU = 2 * NX
LOG2E = math.log2(math.e)
FLOOR = -1e30
PEN = 1e32
WCH = 4
MESH = pl.DeviceIdType.MESH
MIRROR = (0, 2, 1, 4, 3)
BF = jnp.bfloat16
F32 = jnp.float32


def low_of(x):
    return jnp.where(x == 0, 0, jnp.where(x == 1, 2, jnp.where(x == 2, 3, 1)))


def column_of(u):
    a = jnp.minimum(u, NU - 1 - u)
    return jnp.where(a == 0, 0, jnp.where(a == 1, 3, jnp.where(a == 2, 1, 2)))


def slot_of(u):
    return jnp.where(u < NX, 0, 1)


def dev(x, yl, z, yh, c):
    return {"ctx": (x * 2 + yl) * NZ + z, "head": yh * 2 + c}


def kernel(
    q_ref, k_ref, v_ref, w_ref, o_ref,
    vraw, vst, kvbuf, qbuf, s_ref, mx_ref, acc, m_ref, l_ref,
    osend, ssend, orecv, srecv, attsend, att, wbuf,
    sw_s, sw_r, qs_s, qs_r, z_s, z_r, sib_s, sib_r,
    w1_s, w1_r, w2_s, w2_r, w3_s, w3_r, wl, vl,
    os_s, os_r, at_s, at_r, as_s, as_r,
):
    ctx = lax.axis_index("ctx")
    head = lax.axis_index("head")
    x = ctx // (2 * NZ)
    yl = (ctx // NZ) % 2
    z = ctx % NZ
    yh = head // 2
    c = head % 2
    scale = LOG2E / math.sqrt(HD)
    D = functools.partial(dev)
    zp, zm = (z + 1) % NZ, (z + NZ - 1) % NZ

    vcopy = pltpu.make_async_copy(v_ref, vraw, vl)
    vcopy.start()
    barrier = pltpu.get_barrier_semaphore()
    partners = []
    for i in range(1, 4 * NX):
        partners.append(D((x + i // 4) % NX, (yl + (i // 2) % 2) % 2, z, yh, (c + i % 2) % 2))
    for i in range(4):
        partners.append(D(x if i < 2 else NX - 1 - x, i % 2, z, 1 - yh, c))
    partners.append(D(x, 1 - yl, z, 1 - yh, 1 - c))
    rel = [z, zm, zp, (z + NZ - 2) % NZ, (z + 2) % NZ, (z + NZ - 3) % NZ, (z + 3) % NZ,
           (z + NZ - 4) % NZ]
    partners += [D(x, yl, rel[r], yh, c) for r in (1, 2, 3, 4)]
    for p in partners:
        pl.semaphore_signal(barrier, inc=1, device_id=p, device_id_type=MESH)
    vcopy.wait()
    vst[0:HD, :] = vraw[0:HD, :].T
    vst[HD:ROWS, :] = vraw[HD:ROWS, :].T
    pl.semaphore_wait(barrier, len(partners))

    def rcopy(src, dst, ss, rs, to):
        return pltpu.make_async_remote_copy(
            src_ref=src, dst_ref=dst, send_sem=ss, recv_sem=rs, device_id=to, device_id_type=MESH
        )

    sib = D(x, yl, z, yh, 1 - c)
    lo = low_of(x)
    hi = NU - 1 - lo
    mine = 2 * x + yl

    col, slo = column_of(mine), slot_of(mine)
    home = D(col, c, z, yh, slo)
    stays = jnp.logical_and(jnp.logical_and(col == x, c == yl), slo == c)

    def kv_half(slot, zz, half):
        return kvbuf.at[slot, zz, pl.ds(half * ROWS, ROWS), :]

    kcp = rcopy(k_ref, kv_half(slo, z, 0), sw_s.at[0], sw_r.at[0], home)
    vcp = rcopy(vst, kv_half(slo, z, 1), sw_s.at[1], sw_r.at[1], home)
    klc = pltpu.make_async_copy(k_ref, kv_half(slo, z, 0), sw_r.at[0])
    vlc = pltpu.make_async_copy(vst, kv_half(slo, z, 1), sw_r.at[1])

    @pl.when(jnp.logical_not(stays))
    def _():
        kcp.start()
        vcp.start()

    @pl.when(stays)
    def _():
        klc.start()
        vlc.start()

    def q_src(d):
        return q_ref.at[:, pl.ds(d * 2 * HD, 2 * HD)]

    def q_each(remote, local):
        for i in range(NX):
            xt = (col + i) % NX
            for d in range(2):
                want = low_of(xt) <= mine
                here = jnp.logical_and(jnp.logical_and(xt == x, c == yl), c == d)

                @pl.when(jnp.logical_and(want, jnp.logical_not(here)))
                def _(i=i, d=d, xt=xt):
                    remote(rcopy(q_src(d), qbuf.at[mine], qs_s.at[i, d], qs_r.at[mine], D(xt, c, z, yh, d)))

                if local is not None:
                    @pl.when(jnp.logical_and(want, here))
                    def _(d=d):
                        local(pltpu.make_async_copy(q_src(d), qbuf.at[mine], qs_r.at[mine]))

    q_each(lambda cp: cp.start(), lambda cp: cp.start())

    DC = o_ref.shape[1]
    WR = w_ref.shape[0]
    WP = WR // WCH
    gw = yh * 2 + c
    xrow = (1 - yh) * 2 + yl
    yrow = (1 - yh) * 2 + (1 - yl)

    def w1(j, d):
        return rcopy(
            w_ref.at[pl.ds(j * WP, WP), pl.ds(((1 - yh) * 2 + d) * DC, DC)],
            wbuf.at[gw, pl.ds(j * WP, WP), :],
            w1_s.at[j, d], w1_r.at[j], D(x, 1 - yl, z, 1 - yh, d),
        )

    def w1_in(j):
        return rcopy(
            wbuf.at[xrow, pl.ds(j * WP, WP), :], wbuf.at[xrow, pl.ds(j * WP, WP), :],
            w2_s.at[j], w1_r.at[j], D(x, 1 - yl, z, yh, c),
        )

    def w2(j):
        return rcopy(
            wbuf.at[xrow, pl.ds(j * WP, WP), :], wbuf.at[xrow, pl.ds(j * WP, WP), :],
            w2_s.at[j], w2_r.at[j], D(x, 1 - yl, z, yh, c),
        )

    w3 = rcopy(
        w_ref.at[:, pl.ds((yh * 2 + 1 - c) * DC, DC)], wbuf.at[gw], w3_s, w3_r, sib
    )
    wown = pltpu.make_async_copy(w_ref.at[:, pl.ds(gw * DC, DC)], wbuf.at[gw], wl)

    def blk(slot, zz):
        return kvbuf.at[slot, zz]

    def zto(r):
        return D(x, yl, rel[r], yh, c)

    def own_to(r):
        return rcopy(blk(c, z), blk(c, z), z_s.at[r], z_r.at[MIRROR[r]], zto(r))

    def pass_on(r):
        return rcopy(blk(c, rel[r]), blk(c, rel[r]), z_s.at[r + 2], z_r.at[r + 2], zto(5 - r))

    def pass_half(r):
        h = r - 3
        return rcopy(half_of(c, rel[r], h), half_of(c, rel[r], h), z_s.at[r + 4], z_r.at[r + 4],
                     zto(7 - r))

    def tosib(r):
        return rcopy(blk(c, rel[r]), blk(c, rel[r]), sib_s.at[r], sib_r.at[r], sib)

    def half_of(slot, zz, h):
        return kvbuf.at[slot, zz, pl.ds(h * ROWS, ROWS), :]

    def arrive(r):
        if r == 7:
            for h in range(2):
                rcopy(half_of(c, rel[7], h), half_of(c, rel[7], h), z_s.at[0], z_r.at[7 + h], sib).wait_recv()
        else:
            rcopy(blk(c, rel[r]), blk(c, rel[r]), z_s.at[0], z_r.at[r], sib).wait_recv()
        if r in (3, 4):
            pass_on(r).start()
            pass_half(r).start()
        tosib(r).start()

    def sib_arrive(r):
        rcopy(blk(1 - c, rel[r]), blk(1 - c, rel[r]), sib_s.at[r], sib_r.at[r], sib).wait_recv()

    m_ref[...] = jnp.full_like(m_ref, FLOOR)
    l_ref[...] = jnp.zeros_like(l_ref)
    acc[...] = jnp.zeros_like(acc)

    for half in range(2):
        pltpu.make_async_copy(kv_half(c, z, half), kv_half(c, z, half), sw_r.at[half]).wait()
    for r in (3, 4, 1, 2):
        own_to(r).start()
    tosib(0).start()

    @pl.when(c != yl)
    def _():
        for j in range(WCH):
            for d in range(2):
                w1(j, d).start()

    def q_wait(u):
        pltpu.make_async_copy(qbuf.at[u], qbuf.at[u], qs_r.at[u]).wait()

    q_wait(lo)
    q_wait(hi)
    w3.start()
    wown.start()

    def hs(h):
        return slice(h * ROWS, (h + 1) * ROWS)

    def qk(slot, zz, u, h):
        return lax.dot_general(
            kvbuf[slot, zz, 0:ROWS, :], qbuf[u, :, h * HD:(h + 1) * HD],
            (((1,), (1,)), ((), ())), preferred_element_type=F32,
        )

    def vt(slot, zz):
        return jnp.concatenate(
            [kvbuf[slot, zz, ROWS:ROWS + HD, :], kvbuf[slot, zz, ROWS + HD:2 * ROWS, :]], axis=1
        )

    def pv(slot, zz, p):
        return lax.dot_general(
            vt(slot, zz), p.astype(BF), (((1,), (0,)), ((), ())), preferred_element_type=F32
        )

    def fold(a, op):
        return op(a.reshape(a.shape[0] // 8, 8, a.shape[1]), axis=0)

    def diagonal(slot, u):
        key_i = lax.broadcasted_iota(jnp.int32, (ROWS, ROWS), 0)
        qry_i = lax.broadcasted_iota(jnp.int32, (ROWS, ROWS), 1)
        allowed = key_i <= qry_i
        for h in range(2):
            s = jnp.where(allowed, qk(slot, z, u, h) * scale, -PEN)
            m = jnp.max(s, axis=0, keepdims=True)
            p = jnp.exp2(s - m)
            m_ref[u, 0:1, hs(h)] = m
            l_ref[u, :, hs(h)] = fold(p, jnp.sum)
            acc[u, :, hs(h)] = pv(slot, z, p)

    def chunk(slot):
        return jnp.where(slot == 0, lo, hi)

    def pen(slot, zz, u):
        kid = chunk(slot) * NZ + zz
        return jnp.where(kid < u * NZ + z, 0.0, PEN).astype(F32)

    def score(blocks, u, h):
        mx = None
        for b, (slot, zz) in enumerate(blocks):
            s = qk(slot, zz, u, h)
            s_ref[b * ROWS:(b + 1) * ROWS, hs(h)] = s
            top = fold(s, jnp.max) - pen(slot, zz, u)
            mx = top if mx is None else jnp.maximum(mx, top)
        mx_ref[:, hs(h)] = mx

    def absorb(blocks, u, blocks_next, un, h):
        m_old = m_ref[u, 0:1, hs(h)]
        m_new = jnp.maximum(m_old, jnp.max(mx_ref[:, hs(h)], axis=0, keepdims=True) * scale)
        alpha = jnp.exp2(m_old - m_new)
        m_ref[u, 0:1, hs(h)] = m_new
        l8, out = None, None
        for b, (slot, zz) in enumerate(blocks):
            p = jnp.exp2(s_ref[b * ROWS:(b + 1) * ROWS, hs(h)] * scale - (m_new + pen(slot, zz, u)))
            p8 = fold(p, jnp.sum)
            l8 = p8 if l8 is None else l8 + p8
            d = pv(slot, zz, p)
            out = d if out is None else out + d
        score(blocks_next, un, h)
        l_ref[u, :, hs(h)] = l_ref[u, :, hs(h)] * alpha + l8
        acc[u, :, hs(h)] = acc[u, :, hs(h)] * alpha + out

    diagonal(c, chunk(c))
    sib_arrive(0)
    diagonal(1 - c, chunk(1 - c))

    def o_send(u):
        return rcopy(osend.at[u], orecv.at[x, slot_of(u)], os_s.at[u, 0],
                     os_r.at[x, slot_of(u), 0], D(column_of(u), yl, z, yh, c))

    def st_send(u):
        return rcopy(ssend.at[u], srecv.at[x, slot_of(u)], os_s.at[u, 1],
                     os_r.at[x, slot_of(u), 1], D(column_of(u), yl, z, yh, c))

    def w_on(j):
        w1_in(j).wait_recv()
        w2(j).start()

    for r in (3, 4, 1):
        arrive(r)
    for r in (3, 4, 1):
        sib_arrive(r)
    NU1 = NU + 1

    def unit(i):
        j = jnp.where(i < NU1, NU - i, i - NU1)
        u = jnp.where(j < 2 * lo, NU - 1 - j // 2, jnp.where(j < NU - 2, NU - 2 - j + lo, jnp.where(
            j < NU, hi, lo)))
        slot = jnp.where(j < 2 * lo, 1 - j % 2, jnp.where(j == NU - 2, 1, 0))
        zs = [jnp.where(i < NU1, rel[r0], rel[r1]) for r0, r1 in ((0, 2), (3, 5), (4, 6), (1, 7))]
        return u, slot, [(slot, zz) for zz in zs]

    def begin(_):
        u, _, blocks = unit(jnp.int32(0))
        for h in range(2):
            score(blocks, u, h)

    begin(0)

    def one(i, _):
        u, slot, blocks = unit(i)
        un, _, blocks_n = unit(jnp.minimum(i + 1, 2 * NU1 - 1))

        @pl.when(i == 3)
        def _():
            arrive(2)

        @pl.when(i == 6)
        def _():
            for r in (5, 6, 7):
                arrive(r)

        @pl.when(i == 8)
        def _():
            for r in (2, 5, 6, 7):
                sib_arrive(r)
            w_on(0)

        for k, at in ((1, 12), (2, 15)):
            @pl.when(i == at)
            def _():
                w_on(k)

        @pl.when(jnp.logical_and(jnp.logical_and(i < NU, un != u), jnp.logical_and(un != lo, un != hi)))
        def _():
            q_wait(un)

        for h in range(2):
            absorb(blocks, u, blocks_n, un, h)

        @pl.when(jnp.logical_and(jnp.logical_and(i >= NU1, slot == 0), jnp.logical_and(u != lo, u != hi)))
        def _():
            osend[u] = acc[u].astype(BF)
            lsum = jnp.sum(l_ref[u], axis=0, keepdims=True)
            ssend[u] = jnp.concatenate(
                [jnp.broadcast_to(m_ref[u, 0:1, :], (4, 2 * ROWS)),
                 jnp.broadcast_to(lsum, (4, 2 * ROWS))], axis=0)
            o_send(u).start()
            st_send(u).start()

        return 0

    lax.fori_loop(0, 2 * NU1, one, 0)
    w_on(3)

    g = yh * 2 + yl

    def chunk_of(s):
        return lo if s == 0 else hi

    def owner(s, t):
        u = chunk_of(s)
        return D(u // 2, u % 2, z, t, c)

    def owned(s, t):
        u = chunk_of(s)
        return jnp.logical_and(u == mine, yh == t)

    def a_remote(s, t):
        return rcopy(attsend.at[s], att.at[g, c], at_s.at[s, t], at_r.at[g], owner(s, t))

    def a_local(s):
        return pltpu.make_async_copy(attsend.at[s], att.at[g, c], at_r.at[g])

    for s in (1, 0):
        u = chunk_of(s)
        l_ref[u, 0:1, :] = jnp.sum(l_ref[u], axis=0, keepdims=True)

        def merge(xs, s=s, u=u):
            rcopy(osend.at[u], orecv.at[xs, s], os_s.at[u, 0], os_r.at[xs, s, 0], sib).wait_recv()
            rcopy(ssend.at[u], srecv.at[xs, s], os_s.at[u, 1], os_r.at[xs, s, 1], sib).wait_recv()
            m_old = m_ref[u, 0:1, :]
            m_in = srecv[xs, s, 0:1, :]
            m_new = jnp.maximum(m_old, m_in)
            a_old = jnp.exp2(m_old - m_new)
            a_in = jnp.exp2(m_in - m_new)
            m_ref[u, 0:1, :] = m_new
            l_ref[u, 0:1, :] = l_ref[u, 0:1, :] * a_old + srecv[xs, s, 4:5, :] * a_in
            acc[u] = acc[u] * a_old + orecv[xs, s].astype(F32) * a_in

        for xs in range(NX):
            pl.when(jnp.logical_and(xs != x, low_of(xs) <= u))(functools.partial(merge, xs))
        for h in range(2):
            o = acc[u, :, hs(h)] / l_ref[u, 0:1, hs(h)]
            attsend[s, :, h * HD:(h + 1) * HD] = o.T.astype(BF)
        for t in range(2):
            here = owned(s, t)

            @pl.when(here)
            def _():
                a_local(s).start()

            @pl.when(jnp.logical_not(here))
            def _():
                a_remote(s, t).start()

    def a_sib(gg):
        return rcopy(att.at[gg, c], att.at[gg, c], as_s.at[gg], as_r.at[gg], sib)

    for gg in range(4):
        pltpu.make_async_copy(attsend.at[0], att.at[gg, c], at_r.at[gg]).wait()
        a_sib(gg).start()
    w3.wait_recv()
    wown.wait()
    for j in range(WCH):
        rcopy(wbuf.at[yrow, pl.ds(j * WP, WP), :], wbuf.at[yrow, pl.ds(j * WP, WP), :],
              w2_s.at[j], w2_r.at[j], sib).wait_recv()
    for gg in range(4):
        rcopy(att.at[gg, 1 - c], att.at[gg, 1 - c], as_s.at[gg], as_r.at[gg], sib).wait_recv()

    rows = jnp.concatenate([att[i // 2, i % 2] for i in range(8)], axis=1)
    for j in range(DC // 256):
        cs = slice(j * 256, (j + 1) * 256)
        wcol = jnp.concatenate([wbuf[i, :, cs] for i in range(4)], axis=0)
        o_ref[:, cs] = jnp.dot(rows, wcol, preferred_element_type=F32).astype(BF)

    @pl.when(jnp.logical_not(stays))
    def _():
        kcp.wait_send()
        vcp.wait_send()

    q_each(lambda cp: cp.wait_send(), None)

    @pl.when(c != yl)
    def _():
        for j in range(WCH):
            for d in range(2):
                w1(j, d).wait_send()
    for j in range(WCH):
        w2(j).wait_send()
    w3.wait_send()
    for r in (1, 2, 3, 4):
        own_to(r).wait_send()
    for r in (3, 4):
        pass_on(r).wait_send()
        pass_half(r).wait_send()
    for r in range(8):
        tosib(r).wait_send()

    def sent(u, _):
        @pl.when(jnp.logical_and(u != lo, u != hi))
        def _():
            o_send(u).wait_send()
            st_send(u).wait_send()

        return 0

    lax.fori_loop(lo, NU, sent, 0)
    for s in range(2):
        for t in range(2):
            @pl.when(jnp.logical_not(owned(s, t)))
            def _():
                a_remote(s, t).wait_send()
    for gg in range(4):
        a_sib(gg).wait_send()


def per_device(query, keys, values, out_weight):
    rows = query.shape[0]
    d_model = out_weight.shape[1]
    dma = pltpu.SemaphoreType.DMA
    vm = pl.BlockSpec(memory_space=pltpu.VMEM)
    hbm = pl.BlockSpec(memory_space=pltpu.HBM)
    R2 = 2 * ROWS
    return pl.pallas_call(
        kernel,
        out_shape=jax.ShapeDtypeStruct((rows, d_model // 4), BF),
        in_specs=[hbm, hbm, hbm, hbm],
        out_specs=vm,
        scratch_shapes=[
            pltpu.VMEM((ROWS, HD), BF),
            pltpu.VMEM((ROWS, HD), BF),
            pltpu.VMEM((2, NZ, R2, HD), BF),
            pltpu.VMEM((NU, ROWS, 2 * HD), BF),
            pltpu.VMEM((4 * ROWS, R2), F32),
            pltpu.VMEM((8, R2), F32),
            pltpu.VMEM((NU, HD, R2), F32),
            pltpu.VMEM((NU, 8, R2), F32),
            pltpu.VMEM((NU, 8, R2), F32),
            pltpu.VMEM((NU, HD, R2), BF),
            pltpu.VMEM((NU, 8, R2), F32),
            pltpu.VMEM((NX, 2, HD, R2), BF),
            pltpu.VMEM((NX, 2, 8, R2), F32),
            pltpu.VMEM((2, ROWS, 2 * HD), BF),
            pltpu.VMEM((4, 2, ROWS, 2 * HD), BF),
            pltpu.VMEM((4, out_weight.shape[0], d_model // 4), BF),
            dma((2,)), dma((2,)),
            dma((NX, 2)), dma((NU,)),
            dma((9,)), dma((9,)),
            dma((8,)), dma((8,)),
            dma((WCH, 2)), dma((WCH,)), dma((WCH,)), dma((WCH,)), dma, dma, dma, dma,
            dma((NU, 2)), dma((NX, 2, 2)),
            dma((2, 2)), dma((4,)), dma((4,)), dma((4,)),
        ],
        compiler_params=pltpu.CompilerParams(
            collective_id=0, has_side_effects=True, vmem_limit_bytes=48 * 1024 * 1024
        ),
    )(query, keys, values, out_weight)


def solution(mesh):
    return jax.shard_map(
        per_device,
        mesh=mesh,
        in_specs=(P("ctx", "head"), P("ctx", "head"), P("ctx", "head"), P("head", None)),
        out_specs=P("ctx", "head"),
        check_vma=False,
    )
```

```python
import functools
import math

import jax
import jax.numpy as jnp
from jax import lax
from jax.experimental import pallas as pl
from jax.experimental.pallas import tpu as pltpu
from jax.sharding import PartitionSpec as P

HD = 128
ROWS = 256
NX, NZ = 4, 8
NU = 2 * NX
LOG2E = math.log2(math.e)
FLOOR = -1e30
PEN = 1e32
WCH = 4
MESH = pl.DeviceIdType.MESH
MIRROR = (0, 2, 1, 4, 3)
BF = jnp.bfloat16
F32 = jnp.float32


def low_of(x):
    return 2 * x


def column_of(u):
    return u // 2


def slot_of(u):
    return u % 2


def dev(x, yl, z, yh, c):
    return {"ctx": (x * 2 + yl) * NZ + z, "head": yh * 2 + c}


def kernel(
    q_ref, k_ref, v_ref, w_ref, o_ref,
    vraw, vst, kvbuf, qbuf, s_ref, mx_ref, acc, m_ref, l_ref,
    osend, ssend, orecv, srecv, attsend, att, wbuf,
    sw_s, sw_r, qs_s, qs_r, z_s, z_r, sib_s, sib_r,
    w1_s, w1_r, w2_s, w2_r, w3_s, w3_r, wl, vl,
    os_s, os_r, at_s, at_r, as_s, as_r,
):
    ctx = lax.axis_index("ctx")
    head = lax.axis_index("head")
    x = ctx // (2 * NZ)
    yl = (ctx // NZ) % 2
    z = ctx % NZ
    yh = head // 2
    c = head % 2
    scale = LOG2E / math.sqrt(HD)
    D = functools.partial(dev)
    zp, zm = (z + 1) % NZ, (z + NZ - 1) % NZ

    vcopy = pltpu.make_async_copy(v_ref, vraw, vl)
    vcopy.start()
    barrier = pltpu.get_barrier_semaphore()
    partners = []
    for i in range(1, 4 * NX):
        partners.append(D((x + i // 4) % NX, (yl + (i // 2) % 2) % 2, z, yh, (c + i % 2) % 2))
    for i in range(2):
        partners.append(D(x, i, z, 1 - yh, c))
    partners.append(D(x, 1 - yl, z, 1 - yh, 1 - c))
    rel = [z, zm, zp, (z + NZ - 2) % NZ, (z + 2) % NZ, (z + NZ - 3) % NZ, (z + 3) % NZ,
           (z + NZ - 4) % NZ]
    partners += [D(x, yl, rel[r], yh, c) for r in (1, 2, 3, 4)]
    for p in partners:
        pl.semaphore_signal(barrier, inc=1, device_id=p, device_id_type=MESH)
    vcopy.wait()
    vst[0:HD, :] = vraw[0:HD, :].T
    vst[HD:ROWS, :] = vraw[HD:ROWS, :].T
    pl.semaphore_wait(barrier, len(partners))

    def rcopy(src, dst, ss, rs, to):
        return pltpu.make_async_remote_copy(
            src_ref=src, dst_ref=dst, send_sem=ss, recv_sem=rs, device_id=to, device_id_type=MESH
        )

    sib = D(x, yl, z, yh, 1 - c)
    lo = low_of(x)
    hi = lo + 1
    top = jnp.where(x == 0, NU - 3, NU - 1)
    at_end = x == NX - 1
    mine = 2 * x + yl

    col, slo = column_of(mine), slot_of(mine)
    home = D(col, c, z, yh, slo)
    stays = jnp.logical_and(jnp.logical_and(col == x, c == yl), slo == c)

    def kv_half(slot, zz, half):
        return kvbuf.at[slot, zz, pl.ds(half * ROWS, ROWS), :]

    kcp = rcopy(k_ref, kv_half(slo, z, 0), sw_s.at[0], sw_r.at[0], home)
    vcp = rcopy(vst, kv_half(slo, z, 1), sw_s.at[1], sw_r.at[1], home)
    klc = pltpu.make_async_copy(k_ref, kv_half(slo, z, 0), sw_r.at[0])
    vlc = pltpu.make_async_copy(vst, kv_half(slo, z, 1), sw_r.at[1])

    home2 = D(NX - 1, c, z, yh, slo)
    kcp2 = rcopy(k_ref, kv_half(2 + slo, z, 0), sw_s.at[2], sw_r.at[2], home2)
    vcp2 = rcopy(vst, kv_half(2 + slo, z, 1), sw_s.at[3], sw_r.at[3], home2)

    @pl.when(jnp.logical_not(stays))
    def _():
        kcp.start()
        vcp.start()

    @pl.when(x == 0)
    def _():
        kcp2.start()
        vcp2.start()

    @pl.when(stays)
    def _():
        klc.start()
        vlc.start()

    def q_src(d):
        return q_ref.at[:, pl.ds(d * 2 * HD, 2 * HD)]

    def q_each(remote, local):
        for i in range(NX):
            xt = (col + i) % NX
            for d in range(2):
                want = jnp.logical_and(low_of(xt) <= mine, jnp.logical_or(xt > 0, mine < NU - 2))
                here = jnp.logical_and(jnp.logical_and(xt == x, c == yl), c == d)

                @pl.when(jnp.logical_and(want, jnp.logical_not(here)))
                def _(i=i, d=d, xt=xt):
                    remote(rcopy(q_src(d), qbuf.at[mine], qs_s.at[i, d], qs_r.at[mine], D(xt, c, z, yh, d)))

                if local is not None:
                    @pl.when(jnp.logical_and(want, here))
                    def _(d=d):
                        local(pltpu.make_async_copy(q_src(d), qbuf.at[mine], qs_r.at[mine]))


    DC = o_ref.shape[1]
    WR = w_ref.shape[0]
    WP = WR // WCH
    gw = yh * 2 + c
    xrow = (1 - yh) * 2 + yl
    yrow = (1 - yh) * 2 + (1 - yl)

    def w1(j, d):
        return rcopy(
            w_ref.at[pl.ds(j * WP, WP), pl.ds(((1 - yh) * 2 + d) * DC, DC)],
            wbuf.at[gw, pl.ds(j * WP, WP), :],
            w1_s.at[j, d], w1_r.at[j], D(x, 1 - yl, z, 1 - yh, d),
        )

    def w1_in(j):
        return rcopy(
            wbuf.at[xrow, pl.ds(j * WP, WP), :], wbuf.at[xrow, pl.ds(j * WP, WP), :],
            w2_s.at[j], w1_r.at[j], D(x, 1 - yl, z, yh, c),
        )

    def w2(j):
        return rcopy(
            wbuf.at[xrow, pl.ds(j * WP, WP), :], wbuf.at[xrow, pl.ds(j * WP, WP), :],
            w2_s.at[j], w2_r.at[j], D(x, 1 - yl, z, yh, c),
        )

    w3 = rcopy(
        w_ref.at[:, pl.ds((yh * 2 + 1 - c) * DC, DC)], wbuf.at[gw], w3_s, w3_r, sib
    )
    wown = pltpu.make_async_copy(w_ref.at[:, pl.ds(gw * DC, DC)], wbuf.at[gw], wl)

    def blk(slot, zz):
        return kvbuf.at[slot, zz]

    def zto(r):
        return D(x, yl, rel[r], yh, c)

    def half_of(slot, zz, h):
        return kvbuf.at[slot, zz, pl.ds(h * ROWS, ROWS), :]

    def own_to(r, h, e=0):
        src = half_of(2 * e + c, z, h)
        return rcopy(src, src, z_s.at[e, r, h], z_r.at[e, MIRROR[r], h], zto(r))

    def pass_on(r, h, e=0):
        src = half_of(2 * e + c, rel[r], h)
        return rcopy(src, src, z_s.at[e, r + 2, h], z_r.at[e, r + 2, h], zto(5 - r))

    def pass_half(r, e=0):
        src = half_of(2 * e + c, rel[r], r - 3)
        return rcopy(src, src, z_s.at[e, 7, r - 3], z_r.at[e, 7, r - 3], zto(7 - r))

    def tosib(r, e=0):
        src = blk(2 * e + c, rel[r])
        return rcopy(src, src, sib_s.at[e, r], sib_r.at[e, r], sib)

    def landed(r, h, e):
        src = half_of(2 * e + c, rel[r], h)
        rcopy(src, src, z_s.at[e, 0, 0], z_r.at[e, r, h], sib).wait_recv()

    def arrive(r, e=0):
        for h in range(2):
            landed(r, h, e)
        tosib(r, e).start()

    def arrive_two(e=0):
        for h in range(2):
            for r in (3, 4):
                landed(r, h, e)
                pass_on(r, h, e).start()
                if h == r - 3:
                    pass_half(r, e).start()
        for r in (3, 4):
            tosib(r, e).start()

    def sib_arrive(r, e=0):
        src = blk(2 * e + 1 - c, rel[r])
        rcopy(src, src, sib_s.at[e, r], sib_r.at[e, r], sib).wait_recv()

    def launch_two(e):
        for h in range(2):
            src = half_of(2 * e + c, z, h)
            pltpu.make_async_copy(src, src, sw_r.at[2 * e + h]).wait()
            for r in (3, 4):
                own_to(r, h, e).start()
        tosib(0, e).start()

    def launch_one(e):
        for h in range(2):
            for r in (3, 4):
                own_to(r, h, e).wait_send()
            for r in (1, 2):
                own_to(r, h, e).start()

    def drained(e):
        for h in range(2):
            for r in (1, 2):
                own_to(r, h, e).wait_send()
            for r in (3, 4):
                pass_on(r, h, e).wait_send()
        for r in (3, 4):
            pass_half(r, e).wait_send()
        for r in range(8):
            tosib(r, e).wait_send()

    @pl.when(c != yl)
    def _():
        for j in range(WCH):
            for d in range(2):
                w1(j, d).start()

    q_each(lambda cp: cp.start(), lambda cp: cp.start())
    m_ref[...] = jnp.full_like(m_ref, FLOOR)
    l_ref[...] = jnp.zeros_like(l_ref)
    acc[...] = jnp.zeros_like(acc)

    launch_two(0)

    def q_wait(u):
        pltpu.make_async_copy(qbuf.at[u], qbuf.at[u], qs_r.at[u]).wait()

    q_wait(lo)
    q_wait(hi)
    w3.start()
    wown.start()

    def hs(h):
        return slice(h * ROWS, (h + 1) * ROWS)

    def qk(slot, zz, u, h):
        return lax.dot_general(
            kvbuf[slot, zz, 0:ROWS, :], qbuf[u, :, h * HD:(h + 1) * HD],
            (((1,), (1,)), ((), ())), preferred_element_type=F32,
        )

    def vt(slot, zz):
        return jnp.concatenate(
            [kvbuf[slot, zz, ROWS:ROWS + HD, :], kvbuf[slot, zz, ROWS + HD:2 * ROWS, :]], axis=1
        )

    def pv(slot, zz, p):
        return lax.dot_general(
            vt(slot, zz), p.astype(BF), (((1,), (0,)), ((), ())), preferred_element_type=F32
        )

    def fold(a, op):
        return op(a.reshape(a.shape[0] // 8, 8, a.shape[1]), axis=0)

    def diagonal(slot, u):
        key_i = lax.broadcasted_iota(jnp.int32, (ROWS, ROWS), 0)
        qry_i = lax.broadcasted_iota(jnp.int32, (ROWS, ROWS), 1)
        allowed = key_i <= qry_i
        for h in range(2):
            s = jnp.where(allowed, qk(slot, z, u, h) * scale, -PEN)
            m = jnp.max(s, axis=0, keepdims=True)
            p = jnp.exp2(s - m)
            m_ref[u, 0:1, hs(h)] = m
            l_ref[u, :, hs(h)] = fold(p, jnp.sum)
            acc[u, :, hs(h)] = pv(slot, z, p)

    def chunk(slot):
        return jnp.where(slot < 2, lo + slot, slot - 2)

    def pen(slot, zz, u):
        kid = chunk(slot) * NZ + zz
        return jnp.where(kid < u * NZ + z, 0.0, PEN).astype(F32)

    def score(blocks, u, h):
        mx = None
        for b, (slot, zz) in enumerate(blocks):
            s = qk(slot, zz, u, h)
            s_ref[b * ROWS:(b + 1) * ROWS, hs(h)] = s
            top = fold(s, jnp.max) - pen(slot, zz, u)
            mx = top if mx is None else jnp.maximum(mx, top)
        mx_ref[:, hs(h)] = mx

    def absorb(blocks, u, blocks_next, un, h):
        m_old = m_ref[u, 0:1, hs(h)]
        m_new = jnp.maximum(m_old, jnp.max(mx_ref[:, hs(h)], axis=0, keepdims=True) * scale)
        alpha = jnp.exp2(m_old - m_new)
        m_ref[u, 0:1, hs(h)] = m_new
        l8, out = None, None
        for b, (slot, zz) in enumerate(blocks):
            p = jnp.exp2(s_ref[b * ROWS:(b + 1) * ROWS, hs(h)] * scale - (m_new + pen(slot, zz, u)))
            p8 = fold(p, jnp.sum)
            l8 = p8 if l8 is None else l8 + p8
            d = pv(slot, zz, p)
            out = d if out is None else out + d
        score(blocks_next, un, h)
        l_ref[u, :, hs(h)] = l_ref[u, :, hs(h)] * alpha + l8
        acc[u, :, hs(h)] = acc[u, :, hs(h)] * alpha + out

    diagonal(c, chunk(c))
    launch_one(0)
    sib_arrive(0)
    diagonal(1 - c, chunk(1 - c))

    @pl.when(at_end)
    def _():
        launch_two(1)

    def o_send(u):
        return rcopy(osend.at[u], orecv.at[x, slot_of(u)], os_s.at[u, 0],
                     os_r.at[x, slot_of(u), 0], D(column_of(u), yl, z, yh, c))

    def st_send(u):
        return rcopy(ssend.at[u], srecv.at[x, slot_of(u)], os_s.at[u, 1],
                     os_r.at[x, slot_of(u), 1], D(column_of(u), yl, z, yh, c))

    g = yh * 2 + yl

    def chunk_of(s):
        return lo if s == 0 else hi

    def owner(s, t):
        u = chunk_of(s)
        return D(u // 2, u % 2, z, t, c)

    def owned(s, t):
        u = chunk_of(s)
        return jnp.logical_and(u == mine, yh == t)

    def a_remote(s, t):
        return rcopy(attsend.at[s], att.at[g, c], at_s.at[s, t], at_r.at[g], owner(s, t))

    def a_local(s):
        return pltpu.make_async_copy(attsend.at[s], att.at[g, c], at_r.at[g])

    def finish(s):
        u = chunk_of(s)
        l_ref[u, 0:1, :] = jnp.sum(l_ref[u], axis=0, keepdims=True)

        def merge(xs, s=s, u=u):
            rcopy(osend.at[u], orecv.at[xs, s], os_s.at[u, 0], os_r.at[xs, s, 0], sib).wait_recv()
            rcopy(ssend.at[u], srecv.at[xs, s], os_s.at[u, 1], os_r.at[xs, s, 1], sib).wait_recv()
            m_old = m_ref[u, 0:1, :]
            m_in = srecv[xs, s, 0:1, :]
            m_new = jnp.maximum(m_old, m_in)
            a_old = jnp.exp2(m_old - m_new)
            a_in = jnp.exp2(m_in - m_new)
            m_ref[u, 0:1, :] = m_new
            l_ref[u, 0:1, :] = l_ref[u, 0:1, :] * a_old + srecv[xs, s, 4:5, :] * a_in
            acc[u] = acc[u] * a_old + orecv[xs, s].astype(F32) * a_in

        for xs in range(NX):
            there = xs < x if xs > 0 else jnp.logical_and(x > 0, x < NX - 1)
            pl.when(there)(functools.partial(merge, xs))
        for h in range(2):
            o = acc[u, :, hs(h)] / l_ref[u, 0:1, hs(h)]
            attsend[s, :, h * HD:(h + 1) * HD] = o.T.astype(BF)
        for t in range(2):
            here = owned(s, t)

            @pl.when(here)
            def _():
                a_local(s).start()

            @pl.when(jnp.logical_not(here))
            def _():
                a_remote(s, t).start()

    def w_on(j):
        w1_in(j).wait_recv()
        w2(j).start()

    def events(seg):
        if seg == 0:
            arrive_two()
            w_on(0)
            sib_arrive(3)
        if seg == 1:
            arrive(1)
            arrive(2)
            pl.when(at_end)(functools.partial(launch_one, 1))
            w_on(1)
        if seg == 2:
            sib_arrive(1)
            sib_arrive(4)

            @pl.when(at_end)
            def _():
                arrive_two(1)

            w_on(2)
        if seg == 3:
            arrive(5)
            arrive(6)
            arrive(7)
        if seg == 4:
            for r in (2, 5, 6, 7):
                sib_arrive(r)
            w_on(3)
        if seg == 6:
            @pl.when(at_end)
            def _():
                for r in (1, 2, 5, 6, 7):
                    arrive(r, 1)
                for r in range(8):
                    sib_arrive(r, 1)

    groups = ((0, 3), (1, 4), (2, 5), (6, 7))

    def zpick(k, r0):
        return jnp.where(k == 0, rel[r0[0]], jnp.where(k == 1, rel[r0[1]], jnp.where(
            k == 2, rel[r0[2]], rel[r0[3]])))

    def group(k, base):
        za = zpick(k, [gr[0] for gr in groups])
        zb = zpick(k, [gr[1] for gr in groups])
        return [(base, za), (base + 1, za), (base, zb), (base + 1, zb)]

    n = top - lo + 1
    far = top - hi

    def pick(seg, *values):
        out = values[-1]
        for e in range(len(values) - 2, -1, -1):
            out = jnp.where(seg == e, values[e], out)
        return out

    def segment(seg, _):
        for e in (0, 1, 2, 3, 4, 6):
            pl.when(seg == e)(functools.partial(events, e))
        first = pick(seg, 0, n // 2, 0, far // 2, 0, 0, 0)
        end = pick(seg, n // 2, n, far // 2, far, 2 * far, 6, jnp.where(at_end, 8, 0))
        count = pick(seg, n, n, far, far, 2 * far, 6, 8)
        base = jnp.where(seg == 6, 2, 0)

        def at(i):
            return pick(seg, lo + i, lo + i, hi + 1 + i, hi + 1 + i, top - i // 2,
                        hi - i // 3, hi - i // 4)

        def grp(i):
            return group(pick(seg, 0, 0, 1, 1, 2 + i % 2, 1 + i % 3, i % 4), base)

        @pl.when(jnp.logical_and(first == 0, end > 0))
        def _():
            for h in range(2):
                score(grp(0), at(0), h)

        def one(i, _):
            u = at(i)
            nxt = jnp.minimum(i + 1, count - 1)
            un = at(nxt)

            @pl.when(jnp.logical_and(seg < 2, jnp.logical_and(un > u, un > hi)))
            def _():
                q_wait(un)

            for h in range(2):
                absorb(grp(i), u, grp(nxt), un, h)

            @pl.when(jnp.logical_and(seg == 4, i % 2 == 1))
            def _():
                osend[u] = acc[u].astype(BF)
                lsum = jnp.sum(l_ref[u], axis=0, keepdims=True)
                ssend[u] = jnp.concatenate(
                    [jnp.broadcast_to(m_ref[u, 0:1, :], (4, 2 * ROWS)),
                     jnp.broadcast_to(lsum, (4, 2 * ROWS))], axis=0)
                o_send(u).start()
                st_send(u).start()

            complete = jnp.where(at_end, jnp.logical_and(seg == 6, i == 3),
                                 jnp.logical_and(seg == 5, i == 2))

            @pl.when(complete)
            def _():
                finish(1)

            return 0

        lax.fori_loop(first, end, one, 0)
        return 0

    lax.fori_loop(0, 7, segment, 0)
    finish(0)

    def a_sib(gg):
        return rcopy(att.at[gg, c], att.at[gg, c], as_s.at[gg], as_r.at[gg], sib)

    for gg in range(4):
        pltpu.make_async_copy(attsend.at[0], att.at[gg, c], at_r.at[gg]).wait()
        a_sib(gg).start()
    w3.wait_recv()
    wown.wait()
    for j in range(WCH):
        rcopy(wbuf.at[yrow, pl.ds(j * WP, WP), :], wbuf.at[yrow, pl.ds(j * WP, WP), :],
              w2_s.at[j], w2_r.at[j], sib).wait_recv()
    for gg in range(4):
        rcopy(att.at[gg, 1 - c], att.at[gg, 1 - c], as_s.at[gg], as_r.at[gg], sib).wait_recv()

    rows = jnp.concatenate([att[i // 2, i % 2] for i in range(8)], axis=1)
    for j in range(DC // 256):
        cs = slice(j * 256, (j + 1) * 256)
        wcol = jnp.concatenate([wbuf[i, :, cs] for i in range(4)], axis=0)
        o_ref[:, cs] = jnp.dot(rows, wcol, preferred_element_type=F32).astype(BF)

    @pl.when(jnp.logical_not(stays))
    def _():
        kcp.wait_send()
        vcp.wait_send()

    @pl.when(x == 0)
    def _():
        kcp2.wait_send()
        vcp2.wait_send()

    q_each(lambda cp: cp.wait_send(), None)

    @pl.when(c != yl)
    def _():
        for j in range(WCH):
            for d in range(2):
                w1(j, d).wait_send()
    for j in range(WCH):
        w2(j).wait_send()
    w3.wait_send()
    drained(0)

    @pl.when(at_end)
    def _():
        drained(1)

    def sent(u, _):
        o_send(u).wait_send()
        st_send(u).wait_send()
        return 0

    lax.fori_loop(hi + 1, top + 1, sent, 0)
    for s in range(2):
        for t in range(2):
            @pl.when(jnp.logical_not(owned(s, t)))
            def _():
                a_remote(s, t).wait_send()
    for gg in range(4):
        a_sib(gg).wait_send()


def per_device(query, keys, values, out_weight):
    rows = query.shape[0]
    d_model = out_weight.shape[1]
    dma = pltpu.SemaphoreType.DMA
    vm = pl.BlockSpec(memory_space=pltpu.VMEM)
    hbm = pl.BlockSpec(memory_space=pltpu.HBM)
    R2 = 2 * ROWS
    return pl.pallas_call(
        kernel,
        out_shape=jax.ShapeDtypeStruct((rows, d_model // 4), BF),
        in_specs=[hbm, hbm, hbm, hbm],
        out_specs=vm,
        scratch_shapes=[
            pltpu.VMEM((ROWS, HD), BF),
            pltpu.VMEM((ROWS, HD), BF),
            pltpu.VMEM((4, NZ, R2, HD), BF),
            pltpu.VMEM((NU, ROWS, 2 * HD), BF),
            pltpu.VMEM((4 * ROWS, R2), F32),
            pltpu.VMEM((8, R2), F32),
            pltpu.VMEM((NU, HD, R2), F32),
            pltpu.VMEM((NU, 8, R2), F32),
            pltpu.VMEM((NU, 8, R2), F32),
            pltpu.VMEM((NU, HD, R2), BF),
            pltpu.VMEM((NU, 8, R2), F32),
            pltpu.VMEM((NX, 2, HD, R2), BF),
            pltpu.VMEM((NX, 2, 8, R2), F32),
            pltpu.VMEM((2, ROWS, 2 * HD), BF),
            pltpu.VMEM((4, 2, ROWS, 2 * HD), BF),
            pltpu.VMEM((4, out_weight.shape[0], d_model // 4), BF),
            dma((4,)), dma((4,)),
            dma((NX, 2)), dma((NU,)),
            dma((2, NZ, 2)), dma((2, NZ, 2)),
            dma((2, 8)), dma((2, 8)),
            dma((WCH, 2)), dma((WCH,)), dma((WCH,)), dma((WCH,)), dma, dma, dma, dma,
            dma((NU, 2)), dma((NX, 2, 2)),
            dma((2, 2)), dma((4,)), dma((4,)), dma((4,)),
        ],
        compiler_params=pltpu.CompilerParams(
            collective_id=0, has_side_effects=True, vmem_limit_bytes=48 * 1024 * 1024
        ),
    )(query, keys, values, out_weight)


def solution(mesh):
    return jax.shard_map(
        per_device,
        mesh=mesh,
        in_specs=(P("ctx", "head"), P("ctx", "head"), P("ctx", "head"), P("head", None)),
        out_specs=P("ctx", "head"),
        check_vma=False,
    )
```

```python
import functools
import math

import jax
import jax.numpy as jnp
from jax import lax
from jax.experimental import pallas as pl
from jax.experimental.pallas import tpu as pltpu
from jax.sharding import PartitionSpec as P

HD = 128
ROWS = 256
NX, NZ = 4, 8
NU = 2 * NX
LOG2E = math.log2(math.e)
FLOOR = -1e30
PEN = 1e32
WCH = 4
MESH = pl.DeviceIdType.MESH
MIRROR = (0, 2, 1, 4, 3)
BF = jnp.bfloat16
F32 = jnp.float32


def low_of(x):
    return 2 * x


def column_of(u):
    return u // 2


def slot_of(u):
    return u % 2


def dev(x, yl, z, yh, c):
    return {"ctx": (x * 2 + yl) * NZ + z, "head": yh * 2 + c}


def kernel(
    q_ref, k_ref, v_ref, w_ref, o_ref,
    vraw, vst, kvbuf, qbuf, s_ref, mx_ref, acc, m_ref, l_ref,
    osend, ssend, orecv, srecv, attsend, att, wbuf, part,
    sw_s, sw_r, qs_s, qs_r, z_s, z_r, sib_s, sib_r,
    w1_s, w1_r, w2_s, w2_r, w3_s, w3_r, wl, vl,
    os_s, os_r, at_s, at_r, as_s, as_r,
):
    ctx = lax.axis_index("ctx")
    head = lax.axis_index("head")
    x = ctx // (2 * NZ)
    yl = (ctx // NZ) % 2
    z = ctx % NZ
    yh = head // 2
    c = head % 2
    scale = LOG2E / math.sqrt(HD)
    D = functools.partial(dev)
    zp, zm = (z + 1) % NZ, (z + NZ - 1) % NZ

    vcopy = pltpu.make_async_copy(v_ref, vraw, vl)
    vcopy.start()
    barrier = pltpu.get_barrier_semaphore()
    partners = []
    for i in range(1, 4 * NX):
        partners.append(D((x + i // 4) % NX, (yl + (i // 2) % 2) % 2, z, yh, (c + i % 2) % 2))
    for i in range(2):
        partners.append(D(x, i, z, 1 - yh, c))
    partners.append(D(x, 1 - yl, z, 1 - yh, 1 - c))
    rel = [z, zm, zp, (z + NZ - 2) % NZ, (z + 2) % NZ, (z + NZ - 3) % NZ, (z + 3) % NZ,
           (z + NZ - 4) % NZ]
    partners += [D(x, yl, rel[r], yh, c) for r in (1, 2, 3, 4)]
    for p in partners:
        pl.semaphore_signal(barrier, inc=1, device_id=p, device_id_type=MESH)
    vcopy.wait()
    vst[0:HD, :] = vraw[0:HD, :].T
    vst[HD:ROWS, :] = vraw[HD:ROWS, :].T
    pl.semaphore_wait(barrier, len(partners))

    def rcopy(src, dst, ss, rs, to):
        return pltpu.make_async_remote_copy(
            src_ref=src, dst_ref=dst, send_sem=ss, recv_sem=rs, device_id=to, device_id_type=MESH
        )

    sib = D(x, yl, z, yh, 1 - c)
    lo = low_of(x)
    hi = lo + 1
    top = jnp.where(x == 0, NU - 3, NU - 1)
    at_end = x == NX - 1
    mine = 2 * x + yl

    col, slo = column_of(mine), slot_of(mine)
    home = D(col, c, z, yh, slo)
    stays = jnp.logical_and(jnp.logical_and(col == x, c == yl), slo == c)

    def kv_half(slot, zz, half):
        return kvbuf.at[slot, zz, pl.ds(half * ROWS, ROWS), :]

    kcp = rcopy(k_ref, kv_half(slo, z, 0), sw_s.at[0], sw_r.at[0], home)
    vcp = rcopy(vst, kv_half(slo, z, 1), sw_s.at[1], sw_r.at[1], home)
    klc = pltpu.make_async_copy(k_ref, kv_half(slo, z, 0), sw_r.at[0])
    vlc = pltpu.make_async_copy(vst, kv_half(slo, z, 1), sw_r.at[1])

    home2 = D(NX - 1, c, z, yh, slo)
    kcp2 = rcopy(k_ref, kv_half(2 + slo, z, 0), sw_s.at[2], sw_r.at[2], home2)
    vcp2 = rcopy(vst, kv_half(2 + slo, z, 1), sw_s.at[3], sw_r.at[3], home2)

    @pl.when(jnp.logical_not(stays))
    def _():
        kcp.start()
        vcp.start()

    @pl.when(x == 0)
    def _():
        kcp2.start()
        vcp2.start()

    @pl.when(stays)
    def _():
        klc.start()
        vlc.start()

    def q_src(d):
        return q_ref.at[:, pl.ds(d * 2 * HD, 2 * HD)]

    def q_each(remote, local, which=range(NX)):
        for i in which:
            xt = (col + i) % NX
            for d in range(2):
                want = jnp.logical_and(low_of(xt) <= mine, jnp.logical_or(xt > 0, mine < NU - 2))
                here = jnp.logical_and(jnp.logical_and(xt == x, c == yl), c == d)

                @pl.when(jnp.logical_and(want, jnp.logical_not(here)))
                def _(i=i, d=d, xt=xt):
                    remote(rcopy(q_src(d), qbuf.at[mine], qs_s.at[i, d], qs_r.at[mine], D(xt, c, z, yh, d)))

                if local is not None:
                    @pl.when(jnp.logical_and(want, here))
                    def _(d=d):
                        local(pltpu.make_async_copy(q_src(d), qbuf.at[mine], qs_r.at[mine]))


    DC = o_ref.shape[1]
    WR = w_ref.shape[0]
    WP = WR // WCH
    gw = yh * 2 + c
    xrow = (1 - yh) * 2 + yl
    yrow = (1 - yh) * 2 + (1 - yl)

    def w1(j, d):
        return rcopy(
            w_ref.at[pl.ds(j * WP, WP), pl.ds(((1 - yh) * 2 + d) * DC, DC)],
            wbuf.at[gw, pl.ds(j * WP, WP), :],
            w1_s.at[j, d], w1_r.at[j], D(x, 1 - yl, z, 1 - yh, d),
        )

    def w1_in(j):
        return rcopy(
            wbuf.at[xrow, pl.ds(j * WP, WP), :], wbuf.at[xrow, pl.ds(j * WP, WP), :],
            w2_s.at[j], w1_r.at[j], D(x, 1 - yl, z, yh, c),
        )

    def w2(j):
        return rcopy(
            wbuf.at[xrow, pl.ds(j * WP, WP), :], wbuf.at[xrow, pl.ds(j * WP, WP), :],
            w2_s.at[j], w2_r.at[j], D(x, 1 - yl, z, yh, c),
        )

    w3 = rcopy(
        w_ref.at[:, pl.ds((yh * 2 + 1 - c) * DC, DC)], wbuf.at[gw], w3_s, w3_r, sib
    )
    wown = pltpu.make_async_copy(w_ref.at[:, pl.ds(gw * DC, DC)], wbuf.at[gw], wl)

    def blk(slot, zz):
        return kvbuf.at[slot, zz]

    def zto(r):
        return D(x, yl, rel[r], yh, c)

    def half_of(slot, zz, h):
        return kvbuf.at[slot, zz, pl.ds(h * ROWS, ROWS), :]

    def own_to(r, h, e=0):
        src = half_of(2 * e + c, z, h)
        return rcopy(src, src, z_s.at[e, r, h], z_r.at[e, MIRROR[r], h], zto(r))

    def pass_on(r, h, e=0):
        src = half_of(2 * e + c, rel[r], h)
        return rcopy(src, src, z_s.at[e, r + 2, h], z_r.at[e, r + 2, h], zto(5 - r))

    def pass_half(r, e=0):
        src = half_of(2 * e + c, rel[r], r - 3)
        return rcopy(src, src, z_s.at[e, 7, r - 3], z_r.at[e, 7, r - 3], zto(7 - r))

    def tosib(r, e=0):
        src = blk(2 * e + c, rel[r])
        return rcopy(src, src, sib_s.at[e, r], sib_r.at[e, r], sib)

    def landed(r, h, e):
        src = half_of(2 * e + c, rel[r], h)
        rcopy(src, src, z_s.at[e, 0, 0], z_r.at[e, r, h], sib).wait_recv()

    def arrive(r, e=0):
        for h in range(2):
            landed(r, h, e)
        tosib(r, e).start()

    def arrive_two(e=0):
        for h in range(2):
            for r in (3, 4):
                landed(r, h, e)
                pass_on(r, h, e).start()
                if h == r - 3:
                    pass_half(r, e).start()
        for r in (3, 4):
            tosib(r, e).start()

    def sib_arrive(r, e=0):
        src = blk(2 * e + 1 - c, rel[r])
        rcopy(src, src, sib_s.at[e, r], sib_r.at[e, r], sib).wait_recv()

    def launch_two(e):
        for h in range(2):
            src = half_of(2 * e + c, z, h)
            pltpu.make_async_copy(src, src, sw_r.at[2 * e + h]).wait()
            for r in (3, 4):
                own_to(r, h, e).start()
        tosib(0, e).start()

    def launch_one(e):
        for h in range(2):
            for r in (3, 4):
                own_to(r, h, e).wait_send()
            for r in (1, 2):
                own_to(r, h, e).start()

    def drained(e):
        for h in range(2):
            for r in (1, 2):
                own_to(r, h, e).wait_send()
            for r in (3, 4):
                pass_on(r, h, e).wait_send()
        for r in (3, 4):
            pass_half(r, e).wait_send()
        for r in range(8):
            tosib(r, e).wait_send()

    @pl.when(c != yl)
    def _():
        for j in range(WCH):
            for d in range(2):
                w1(j, d).start()

    m_ref[...] = jnp.full_like(m_ref, FLOOR)
    l_ref[...] = jnp.zeros_like(l_ref)
    acc[...] = jnp.zeros_like(acc)
    @pl.when(jnp.logical_not(stays))
    def _():
        kcp.wait_send()
        vcp.wait_send()

    q_each(lambda cp: cp.start(), lambda cp: cp.start(), (0,))

    launch_two(0)
    q_each(lambda cp: cp.start(), lambda cp: cp.start(), (1, 2, 3))

    def q_wait(u):
        pltpu.make_async_copy(qbuf.at[u], qbuf.at[u], qs_r.at[u]).wait()

    q_wait(lo)
    q_wait(hi)
    w3.start()
    wown.start()

    def hs(h):
        return slice(h * ROWS, (h + 1) * ROWS)

    def qk(slot, zz, u, h):
        return lax.dot_general(
            kvbuf[slot, zz, 0:ROWS, :], qbuf[u, :, h * HD:(h + 1) * HD],
            (((1,), (1,)), ((), ())), preferred_element_type=F32,
        )

    def vt(slot, zz):
        return jnp.concatenate(
            [kvbuf[slot, zz, ROWS:ROWS + HD, :], kvbuf[slot, zz, ROWS + HD:2 * ROWS, :]], axis=1
        )

    def pv(slot, zz, p):
        return lax.dot_general(
            vt(slot, zz), p.astype(BF), (((1,), (0,)), ((), ())), preferred_element_type=F32
        )

    def fold(a, op):
        return op(a.reshape(a.shape[0] // 8, 8, a.shape[1]), axis=0)

    def diagonal(slot, u):
        key_i = lax.broadcasted_iota(jnp.int32, (ROWS, ROWS), 0)
        qry_i = lax.broadcasted_iota(jnp.int32, (ROWS, ROWS), 1)
        allowed = key_i <= qry_i
        for h in range(2):
            s = jnp.where(allowed, qk(slot, z, u, h) * scale, -PEN)
            m = jnp.max(s, axis=0, keepdims=True)
            p = jnp.exp2(s - m)
            m_ref[u, 0:1, hs(h)] = m
            l_ref[u, :, hs(h)] = fold(p, jnp.sum)
            acc[u, :, hs(h)] = pv(slot, z, p)

    def chunk(slot):
        return jnp.where(slot < 2, lo + slot, slot - 2)

    def pen(slot, zz, u):
        kid = chunk(slot) * NZ + zz
        return jnp.where(kid < u * NZ + z, 0.0, PEN).astype(F32)

    def score(blocks, u, h):
        mx = None
        for b, (slot, zz) in enumerate(blocks):
            s = qk(slot, zz, u, h)
            s_ref[b * ROWS:(b + 1) * ROWS, hs(h)] = s
            top = fold(s, jnp.max) - pen(slot, zz, u)
            mx = top if mx is None else jnp.maximum(mx, top)
        mx_ref[:, hs(h)] = mx

    def absorb(blocks, u, blocks_next, un, h):
        m_old = m_ref[u, 0:1, hs(h)]
        m_new = jnp.maximum(m_old, jnp.max(mx_ref[:, hs(h)], axis=0, keepdims=True) * scale)
        alpha = jnp.exp2(m_old - m_new)
        m_ref[u, 0:1, hs(h)] = m_new
        l8, out = None, None
        for b, (slot, zz) in enumerate(blocks):
            p = jnp.exp2(s_ref[b * ROWS:(b + 1) * ROWS, hs(h)] * scale - (m_new + pen(slot, zz, u)))
            p8 = fold(p, jnp.sum)
            l8 = p8 if l8 is None else l8 + p8
            d = pv(slot, zz, p)
            out = d if out is None else out + d
        score(blocks_next, un, h)
        l_ref[u, :, hs(h)] = l_ref[u, :, hs(h)] * alpha + l8
        acc[u, :, hs(h)] = acc[u, :, hs(h)] * alpha + out

    diagonal(c, chunk(c))
    launch_one(0)
    sib_arrive(0)
    diagonal(1 - c, chunk(1 - c))

    @pl.when(at_end)
    def _():
        launch_two(1)

    def o_send(u):
        return rcopy(osend.at[u], orecv.at[x, slot_of(u)], os_s.at[u, 0],
                     os_r.at[x, slot_of(u), 0], D(column_of(u), yl, z, yh, c))

    def st_send(u):
        return rcopy(ssend.at[u], srecv.at[x, slot_of(u)], os_s.at[u, 1],
                     os_r.at[x, slot_of(u), 1], D(column_of(u), yl, z, yh, c))

    g = yh * 2 + yl

    def chunk_of(s):
        return lo if s == 0 else hi

    def owner(s, t):
        u = chunk_of(s)
        return D(u // 2, u % 2, z, t, c)

    def owned(s, t):
        u = chunk_of(s)
        return jnp.logical_and(u == mine, yh == t)

    def a_remote(s, t):
        return rcopy(attsend.at[s], att.at[g, c], at_s.at[s, t], at_r.at[g], owner(s, t))

    def a_local(s):
        return pltpu.make_async_copy(attsend.at[s], att.at[g, c], at_r.at[g])

    def finish(s):
        u = chunk_of(s)
        l_ref[u, 0:1, :] = jnp.sum(l_ref[u], axis=0, keepdims=True)

        def merge(xs, s=s, u=u):
            rcopy(osend.at[u], orecv.at[xs, s], os_s.at[u, 0], os_r.at[xs, s, 0], sib).wait_recv()
            rcopy(ssend.at[u], srecv.at[xs, s], os_s.at[u, 1], os_r.at[xs, s, 1], sib).wait_recv()
            m_old = m_ref[u, 0:1, :]
            m_in = srecv[xs, s, 0:1, :]
            m_new = jnp.maximum(m_old, m_in)
            a_old = jnp.exp2(m_old - m_new)
            a_in = jnp.exp2(m_in - m_new)
            m_ref[u, 0:1, :] = m_new
            l_ref[u, 0:1, :] = l_ref[u, 0:1, :] * a_old + srecv[xs, s, 4:5, :] * a_in
            acc[u] = acc[u] * a_old + orecv[xs, s].astype(F32) * a_in

        for xs in range(NX):
            there = xs < x if xs > 0 else jnp.logical_and(x > 0, x < NX - 1)
            pl.when(there)(functools.partial(merge, xs))
        for h in range(2):
            o = acc[u, :, hs(h)] * (1.0 / l_ref[u, 0:1, hs(h)])
            attsend[s, :, h * HD:(h + 1) * HD] = o.astype(BF).T
        for t in range(2):
            here = owned(s, t)

            @pl.when(here)
            def _():
                a_local(s).start()

            @pl.when(jnp.logical_not(here))
            def _():
                a_remote(s, t).start()

    def w_on(j):
        w1_in(j).wait_recv()
        w2(j).start()

    n = top - lo + 1
    far = top - hi

    def far_end(go, *args):
        pl.when(at_end)(functools.partial(go, *args))

    def when(cond, *acts):
        @pl.when(cond)
        def _():
            for act in acts:
                act()

    def each(go, rs, e=0):
        return lambda: [go(r, e) for r in rs]

    def unit_loop(count, at, blocks, before, after):
        @pl.when(count > 0)
        def _():
            for h in range(2):
                score(blocks(0), at(0), h)

        def one(i, _):
            u = at(i)
            nxt = jnp.minimum(i + 1, count - 1)
            un = at(nxt)
            before(i, u, un)
            for h in range(2):
                absorb(blocks(i), u, blocks(nxt), un, h)
            after(i, u)
            return 0

        lax.fori_loop(0, count, one, 0)

    def ring(e, _):
        base = 2 * e
        own = e == 0
        extra = jnp.logical_and(e == 1, at_end)
        when(own, arrive_two, lambda: w_on(0), each(sib_arrive, (3,)))
        when(extra, each(arrive, (1, 2), 1), each(sib_arrive, (0, 3), 1))

        def at_first(i):
            return jnp.where(own, lo + i, hi - i)

        def before_first(i, u, un):
            when(jnp.logical_and(own, i == n // 2), each(arrive, (1, 2)),
                 lambda: far_end(launch_one, 1), lambda: w_on(1))
            when(jnp.logical_and(own, jnp.logical_and(un > u, un > hi)), lambda: q_wait(un))

        few = jnp.where(at_end, 2, 0)
        unit_loop(jnp.where(own, n, few), at_first,
                  lambda i: [(base + b, rel[r]) for r in (0, 3) for b in range(2)], before_first, lambda i, u: None)

        def rest(t, _):
            first = jnp.logical_and(own, t == 0)
            last = jnp.logical_and(own, t == 1)
            ends = jnp.logical_and(own, t == 2)
            when(first, each(sib_arrive, (1, 2, 4)), lambda: far_end(arrive_two, 1), lambda: w_on(2))
            when(jnp.logical_and(last, far == 0), each(arrive, (5, 6, 7)))
            when(last, each(sib_arrive, (5, 6, 7)), lambda: pl.when(jnp.logical_not(at_end))(lambda: w_on(3)))
            when(jnp.logical_and(extra, t == 0), each(sib_arrive, (1, 2, 4), 1))
            when(jnp.logical_and(extra, t == 1), each(arrive, (5, 6, 7), 1), each(sib_arrive, (5, 6, 7), 1))

            def at(i):
                return jnp.where(first, hi + 1 + i, jnp.where(last, top - i, jnp.where(ends, hi - i // 2, hi - i)))

            def before(i, u, un):
                when(jnp.logical_and(first, i == far // 2), each(arrive, (5, 6, 7)))
                when(jnp.logical_and(ends, jnp.logical_and(at_end, i == 2)), lambda: w_on(3))

            def after(i, u):
                @pl.when(last)
                def _():
                    osend[u] = acc[u].astype(BF)
                    lsum = jnp.sum(l_ref[u], axis=0, keepdims=True)
                    ssend[u] = jnp.concatenate(
                        [jnp.broadcast_to(m_ref[u, 0:1, :], (4, 2 * ROWS)),
                         jnp.broadcast_to(lsum, (4, 2 * ROWS))], axis=0)
                    o_send(u).start()
                    st_send(u).start()

                complete = jnp.where(at_end, jnp.logical_and(jnp.logical_and(extra, t == 1), i == 0),
                                     jnp.logical_and(ends, i == 1))
                when(complete, lambda: finish(1))

            def blocks(i):
                early = jnp.logical_or(t == 0, jnp.logical_and(t == 2, i % 2 == 0))
                zs = [jnp.where(early, rel[a], rel[b]) for a, b in ((1, 5), (2, 6), (4, 7))]
                return [(base + b, zz) for zz in zs for b in range(2)]

            unit_loop(jnp.where(t == 2, jnp.where(own, 4, 0), jnp.where(own, far, few)), at, blocks, before, after)
            return 0

        lax.fori_loop(0, 3, rest, 0)
        return 0

    lax.fori_loop(0, 2, ring, 0)
    finish(0)

    def a_sib(gg):
        return rcopy(att.at[gg, c], att.at[gg, c], as_s.at[gg], as_r.at[gg], sib)

    for gg in range(4):
        pltpu.make_async_copy(attsend.at[0], att.at[gg, c], at_r.at[gg]).wait()
        a_sib(gg).start()
    w3.wait_recv()
    wown.wait()
    for j in range(WCH):
        rcopy(wbuf.at[yrow, pl.ds(j * WP, WP), :], wbuf.at[yrow, pl.ds(j * WP, WP), :],
              w2_s.at[j], w2_r.at[j], sib).wait_recv()

    KH = 2 * HD

    def project(core, j):
        rows = jnp.concatenate([att[i, core] for i in range(4)], axis=1)
        wcol = jnp.concatenate(
            [wbuf[i, pl.ds(pl.multiple_of(core * KH, KH), KH), j * 256:(j + 1) * 256] for i in range(4)], axis=0)
        return jnp.dot(rows, wcol, preferred_element_type=F32)

    for j in range(DC // 256):
        part[:, j * 256:(j + 1) * 256] = project(c, j)
    for gg in range(4):
        rcopy(att.at[gg, 1 - c], att.at[gg, 1 - c], as_s.at[gg], as_r.at[gg], sib).wait_recv()
    for j in range(DC // 256):
        cs = slice(j * 256, (j + 1) * 256)
        o_ref[:, cs] = (part[:, cs] + project(1 - c, j)).astype(BF)

    @pl.when(x == 0)
    def _():
        kcp2.wait_send()
        vcp2.wait_send()

    q_each(lambda cp: cp.wait_send(), None)

    @pl.when(c != yl)
    def _():
        for j in range(WCH):
            for d in range(2):
                w1(j, d).wait_send()
    for j in range(WCH):
        w2(j).wait_send()
    w3.wait_send()
    drained(0)

    @pl.when(at_end)
    def _():
        drained(1)

    def sent(u, _):
        o_send(u).wait_send()
        st_send(u).wait_send()
        return 0

    lax.fori_loop(hi + 1, top + 1, sent, 0)
    for s in range(2):
        for t in range(2):
            @pl.when(jnp.logical_not(owned(s, t)))
            def _():
                a_remote(s, t).wait_send()
    for gg in range(4):
        a_sib(gg).wait_send()


def per_device(query, keys, values, out_weight):
    rows = query.shape[0]
    d_model = out_weight.shape[1]
    dma = pltpu.SemaphoreType.DMA
    vm = pl.BlockSpec(memory_space=pltpu.VMEM)
    hbm = pl.BlockSpec(memory_space=pltpu.HBM)
    R2 = 2 * ROWS
    return pl.pallas_call(
        kernel,
        out_shape=jax.ShapeDtypeStruct((rows, d_model // 4), BF),
        in_specs=[hbm, hbm, hbm, hbm],
        out_specs=vm,
        scratch_shapes=[
            pltpu.VMEM((ROWS, HD), BF),
            pltpu.VMEM((ROWS, HD), BF),
            pltpu.VMEM((4, NZ, R2, HD), BF),
            pltpu.VMEM((NU, ROWS, 2 * HD), BF),
            pltpu.VMEM((6 * ROWS, R2), F32),
            pltpu.VMEM((8, R2), F32),
            pltpu.VMEM((NU, HD, R2), F32),
            pltpu.VMEM((NU, 8, R2), F32),
            pltpu.VMEM((NU, 8, R2), F32),
            pltpu.VMEM((NU, HD, R2), BF),
            pltpu.VMEM((NU, 8, R2), F32),
            pltpu.VMEM((NX, 2, HD, R2), BF),
            pltpu.VMEM((NX, 2, 8, R2), F32),
            pltpu.VMEM((2, ROWS, 2 * HD), BF),
            pltpu.VMEM((4, 2, ROWS, 2 * HD), BF),
            pltpu.VMEM((4, out_weight.shape[0], d_model // 4), BF),
            pltpu.VMEM((rows, d_model // 4), F32),
            dma((4,)), dma((4,)),
            dma((NX, 2)), dma((NU,)),
            dma((2, NZ, 2)), dma((2, NZ, 2)),
            dma((2, 8)), dma((2, 8)),
            dma((WCH, 2)), dma((WCH,)), dma((WCH,)), dma((WCH,)), dma, dma, dma, dma,
            dma((NU, 2)), dma((NX, 2, 2)),
            dma((2, 2)), dma((4,)), dma((4,)), dma((4,)),
        ],
        compiler_params=pltpu.CompilerParams(
            collective_id=0, has_side_effects=True, vmem_limit_bytes=48 * 1024 * 1024
        ),
    )(query, keys, values, out_weight)


def solution(mesh):
    return jax.shard_map(
        per_device,
        mesh=mesh,
        in_specs=(P("ctx", "head"), P("ctx", "head"), P("ctx", "head"), P("head", None)),
        out_specs=P("ctx", "head"),
        check_vma=False,
    )
```

```python
import functools
import math

import jax
import jax.numpy as jnp
from jax import lax
from jax.experimental import pallas as pl
from jax.experimental.pallas import tpu as pltpu
from jax.sharding import PartitionSpec as P

HD = 128
ROWS = 256
NX, NZ = 4, 8
NU = 2 * NX
LOG2E = math.log2(math.e)
FLOOR = -1e30
PEN = 1e32
WCH = 4
MESH = pl.DeviceIdType.MESH
MIRROR = (0, 2, 1, 4, 3)
BF = jnp.bfloat16
F32 = jnp.float32


def low_of(x):
    return 2 * x


def column_of(u):
    return u // 2


def slot_of(u):
    return u % 2


def dev(x, yl, z, yh, c):
    return {"ctx": (x * 2 + yl) * NZ + z, "head": yh * 2 + c}


def kernel(
    q_ref, k_ref, v_ref, w_ref, o_ref,
    vraw, vst, kvbuf, qbuf, s_ref, mx_ref, acc, m_ref, l_ref,
    osend, ssend, orecv, srecv, attsend, att, wbuf, part,
    sw_s, sw_r, qs_s, qs_r, z_s, z_r, sib_s, sib_r,
    w1_s, w1_r, w2_s, w2_r, w3_s, w3_r, wl, vl,
    os_s, os_r, at_s, at_r, as_s, as_r,
):
    ctx = lax.axis_index("ctx")
    head = lax.axis_index("head")
    x = ctx // (2 * NZ)
    yl = (ctx // NZ) % 2
    z = ctx % NZ
    yh = head // 2
    c = head % 2
    scale = LOG2E / math.sqrt(HD)
    D = functools.partial(dev)
    zp, zm = (z + 1) % NZ, (z + NZ - 1) % NZ

    vcopy = pltpu.make_async_copy(v_ref, vraw, vl)
    vcopy.start()
    barrier = pltpu.get_barrier_semaphore()
    partners = []
    for i in range(1, 4 * NX):
        partners.append(D((x + i // 4) % NX, (yl + (i // 2) % 2) % 2, z, yh, (c + i % 2) % 2))
    for i in range(2):
        partners.append(D(x, i, z, 1 - yh, c))
    partners.append(D(x, 1 - yl, z, 1 - yh, 1 - c))
    rel = [z, zm, zp, (z + NZ - 2) % NZ, (z + 2) % NZ, (z + NZ - 3) % NZ, (z + 3) % NZ,
           (z + NZ - 4) % NZ]
    partners += [D(x, yl, rel[r], yh, c) for r in (1, 2, 3, 4)]
    for p in partners:
        pl.semaphore_signal(barrier, inc=1, device_id=p, device_id_type=MESH)
    vcopy.wait()
    vst[0:HD, :] = vraw[0:HD, :].T
    vst[HD:ROWS, :] = vraw[HD:ROWS, :].T
    pl.semaphore_wait(barrier, len(partners))

    def rcopy(src, dst, ss, rs, to):
        return pltpu.make_async_remote_copy(
            src_ref=src, dst_ref=dst, send_sem=ss, recv_sem=rs, device_id=to, device_id_type=MESH
        )

    sib = D(x, yl, z, yh, 1 - c)
    lo = low_of(x)
    hi = lo + 1
    top = jnp.where(x == 0, NU - 3, NU - 1)
    at_end = x == NX - 1
    mine = 2 * x + yl

    col, slo = column_of(mine), slot_of(mine)
    home = D(col, c, z, yh, slo)
    stays = jnp.logical_and(jnp.logical_and(col == x, c == yl), slo == c)

    def kv_half(slot, zz, half):
        return kvbuf.at[slot, zz, pl.ds(half * ROWS, ROWS), :]

    kcp = rcopy(k_ref, kv_half(slo, z, 0), sw_s.at[0], sw_r.at[0], home)
    vcp = rcopy(vst, kv_half(slo, z, 1), sw_s.at[1], sw_r.at[1], home)
    klc = pltpu.make_async_copy(k_ref, kv_half(slo, z, 0), sw_r.at[0])
    vlc = pltpu.make_async_copy(vst, kv_half(slo, z, 1), sw_r.at[1])

    home2 = D(NX - 1, c, z, yh, slo)
    kcp2 = rcopy(k_ref, kv_half(2 + slo, z, 0), sw_s.at[2], sw_r.at[2], home2)
    vcp2 = rcopy(vst, kv_half(2 + slo, z, 1), sw_s.at[3], sw_r.at[3], home2)

    @pl.when(jnp.logical_not(stays))
    def _():
        kcp.start()
        vcp.start()

    @pl.when(x == 0)
    def _():
        kcp2.start()
        vcp2.start()

    @pl.when(stays)
    def _():
        klc.start()
        vlc.start()

    def q_src(d):
        return q_ref.at[:, pl.ds(d * 2 * HD, 2 * HD)]

    def q_each(remote, local, which=range(NX)):
        for i in which:
            xt = (col + i) % NX
            for d in range(2):
                want = jnp.logical_and(low_of(xt) <= mine, jnp.logical_or(xt > 0, mine < NU - 2))
                here = jnp.logical_and(jnp.logical_and(xt == x, c == yl), c == d)

                @pl.when(jnp.logical_and(want, jnp.logical_not(here)))
                def _(i=i, d=d, xt=xt):
                    remote(rcopy(q_src(d), qbuf.at[mine], qs_s.at[i, d], qs_r.at[mine], D(xt, c, z, yh, d)))

                if local is not None:
                    @pl.when(jnp.logical_and(want, here))
                    def _(d=d):
                        local(pltpu.make_async_copy(q_src(d), qbuf.at[mine], qs_r.at[mine]))


    DC = o_ref.shape[1]
    WR = w_ref.shape[0]
    WP = WR // WCH
    gw = yh * 2 + c
    xrow = (1 - yh) * 2 + yl
    yrow = (1 - yh) * 2 + (1 - yl)

    def w1(j, d):
        return rcopy(
            w_ref.at[pl.ds(j * WP, WP), pl.ds(((1 - yh) * 2 + d) * DC, DC)],
            wbuf.at[gw, pl.ds(j * WP, WP), :],
            w1_s.at[j, d], w1_r.at[j], D(x, 1 - yl, z, 1 - yh, d),
        )

    def w1_in(j):
        return rcopy(
            wbuf.at[xrow, pl.ds(j * WP, WP), :], wbuf.at[xrow, pl.ds(j * WP, WP), :],
            w2_s.at[j], w1_r.at[j], D(x, 1 - yl, z, yh, c),
        )

    def w2(j):
        return rcopy(
            wbuf.at[xrow, pl.ds(j * WP, WP), :], wbuf.at[xrow, pl.ds(j * WP, WP), :],
            w2_s.at[j], w2_r.at[j], D(x, 1 - yl, z, yh, c),
        )

    w3 = rcopy(
        w_ref.at[:, pl.ds((yh * 2 + 1 - c) * DC, DC)], wbuf.at[gw], w3_s, w3_r, sib
    )
    wown = pltpu.make_async_copy(w_ref.at[:, pl.ds(gw * DC, DC)], wbuf.at[gw], wl)

    def blk(slot, zz):
        return kvbuf.at[slot, zz]

    def zto(r):
        return D(x, yl, rel[r], yh, c)

    def half_of(slot, zz, h):
        return kvbuf.at[slot, zz, pl.ds(h * ROWS, ROWS), :]

    def own_to(r, h, e=0):
        src = half_of(2 * e + c, z, h)
        return rcopy(src, src, z_s.at[e, r, h], z_r.at[e, MIRROR[r], h], zto(r))

    def pass_on(r, h, e=0):
        src = half_of(2 * e + c, rel[r], h)
        return rcopy(src, src, z_s.at[e, r + 2, h], z_r.at[e, r + 2, h], zto(5 - r))

    def pass_half(r, e=0):
        src = half_of(2 * e + c, rel[r], r - 3)
        return rcopy(src, src, z_s.at[e, 7, r - 3], z_r.at[e, 7, r - 3], zto(7 - r))

    def tosib(r, e=0):
        src = blk(2 * e + c, rel[r])
        return rcopy(src, src, sib_s.at[e, r], sib_r.at[e, r], sib)

    def landed(r, h, e):
        src = half_of(2 * e + c, rel[r], h)
        rcopy(src, src, z_s.at[e, 0, 0], z_r.at[e, r, h], sib).wait_recv()

    def arrive(r, e=0):
        for h in range(2):
            landed(r, h, e)
        tosib(r, e).start()

    def arrive_two(e=0):
        for h in range(2):
            for r in (3, 4):
                landed(r, h, e)
                pass_on(r, h, e).start()
                if h == r - 3:
                    pass_half(r, e).start()
        for r in (3, 4):
            tosib(r, e).start()

    def sib_arrive(r, e=0):
        src = blk(2 * e + 1 - c, rel[r])
        rcopy(src, src, sib_s.at[e, r], sib_r.at[e, r], sib).wait_recv()

    def launch_two(e):
        for h in range(2):
            src = half_of(2 * e + c, z, h)
            pltpu.make_async_copy(src, src, sw_r.at[2 * e + h]).wait()
            for r in (3, 4):
                own_to(r, h, e).start()
        tosib(0, e).start()

    def launch_one(e):
        for h in range(2):
            for r in (3, 4):
                own_to(r, h, e).wait_send()
            for r in (1, 2):
                own_to(r, h, e).start()

    def drained(e):
        for h in range(2):
            for r in (1, 2):
                own_to(r, h, e).wait_send()
            for r in (3, 4):
                pass_on(r, h, e).wait_send()
        for r in (3, 4):
            pass_half(r, e).wait_send()
        for r in range(8):
            tosib(r, e).wait_send()

    @pl.when(c != yl)
    def _():
        for j in range(WCH):
            for d in range(2):
                w1(j, d).start()

    m_ref[...] = jnp.full_like(m_ref, FLOOR)
    l_ref[...] = jnp.zeros_like(l_ref)
    acc[...] = jnp.zeros_like(acc)
    @pl.when(jnp.logical_not(stays))
    def _():
        kcp.wait_send()
        vcp.wait_send()

    q_each(lambda cp: cp.start(), lambda cp: cp.start(), (0,))

    launch_two(0)
    q_each(lambda cp: cp.start(), lambda cp: cp.start(), (1, 2, 3))

    def q_wait(u):
        pltpu.make_async_copy(qbuf.at[u], qbuf.at[u], qs_r.at[u]).wait()

    q_wait(lo)
    q_wait(hi)
    w3.start()
    wown.start()

    def hs(h):
        return slice(h * ROWS, (h + 1) * ROWS)

    def qk(slot, zz, u, h):
        return lax.dot_general(
            kvbuf[slot, zz, 0:ROWS, :], qbuf[u, :, h * HD:(h + 1) * HD],
            (((1,), (1,)), ((), ())), preferred_element_type=F32,
        )

    def vt(slot, zz):
        return jnp.concatenate(
            [kvbuf[slot, zz, ROWS:ROWS + HD, :], kvbuf[slot, zz, ROWS + HD:2 * ROWS, :]], axis=1
        )

    def pv(slot, zz, p):
        return lax.dot_general(
            vt(slot, zz), p.astype(BF), (((1,), (0,)), ((), ())), preferred_element_type=F32
        )

    def fold(a, op):
        return op(a.reshape(a.shape[0] // 8, 8, a.shape[1]), axis=0)

    def diagonal(slot, u):
        key_i = lax.broadcasted_iota(jnp.int32, (ROWS, ROWS), 0)
        qry_i = lax.broadcasted_iota(jnp.int32, (ROWS, ROWS), 1)
        allowed = key_i <= qry_i
        for h in range(2):
            s = jnp.where(allowed, qk(slot, z, u, h) * scale, -PEN)
            m = jnp.max(s, axis=0, keepdims=True)
            p = jnp.exp2(s - m)
            m_ref[u, 0:1, hs(h)] = m
            l_ref[u, :, hs(h)] = fold(p, jnp.sum)
            acc[u, :, hs(h)] = pv(slot, z, p)

    def chunk(slot):
        return jnp.where(slot < 2, lo + slot, slot - 2)

    def pen(slot, zz, u):
        kid = chunk(slot) * NZ + zz
        return jnp.where(kid < u * NZ + z, 0.0, PEN).astype(F32)

    def score(blocks, u, h):
        mx = None
        for b, (slot, zz) in enumerate(blocks):
            s = qk(slot, zz, u, h)
            s_ref[b * ROWS:(b + 1) * ROWS, hs(h)] = s
            top = fold(s, jnp.max) - pen(slot, zz, u)
            mx = top if mx is None else jnp.maximum(mx, top)
        mx_ref[:, hs(h)] = mx

    def absorb(blocks, u, blocks_next, un, h):
        m_old = m_ref[u, 0:1, hs(h)]
        m_new = jnp.maximum(m_old, jnp.max(mx_ref[:, hs(h)], axis=0, keepdims=True) * scale)
        alpha = jnp.exp2(m_old - m_new)
        m_ref[u, 0:1, hs(h)] = m_new
        l8, out = None, None
        for b, (slot, zz) in enumerate(blocks):
            p = jnp.exp2(s_ref[b * ROWS:(b + 1) * ROWS, hs(h)] * scale - (m_new + pen(slot, zz, u)))
            p8 = fold(p, jnp.sum)
            l8 = p8 if l8 is None else l8 + p8
            d = pv(slot, zz, p)
            out = d if out is None else out + d
        score(blocks_next, un, h)
        l_ref[u, :, hs(h)] = l_ref[u, :, hs(h)] * alpha + l8
        acc[u, :, hs(h)] = acc[u, :, hs(h)] * alpha + out

    diagonal(c, chunk(c))
    launch_one(0)
    sib_arrive(0)
    diagonal(1 - c, chunk(1 - c))

    @pl.when(at_end)
    def _():
        launch_two(1)

    def o_send(u):
        return rcopy(osend.at[u], orecv.at[x, slot_of(u)], os_s.at[u, 0],
                     os_r.at[x, slot_of(u), 0], D(column_of(u), yl, z, yh, c))

    def st_send(u):
        return rcopy(ssend.at[u], srecv.at[x, slot_of(u)], os_s.at[u, 1],
                     os_r.at[x, slot_of(u), 1], D(column_of(u), yl, z, yh, c))

    g = yh * 2 + yl

    def chunk_of(s):
        return lo if s == 0 else hi

    def owner(s, t):
        u = chunk_of(s)
        return D(u // 2, u % 2, z, t, c)

    def owned(s, t):
        u = chunk_of(s)
        return jnp.logical_and(u == mine, yh == t)

    def a_src(s, h):
        return attsend.at[s, :, pl.ds(h * HD, HD)]

    def a_at(gg, core, h):
        return att.at[gg, core, :, pl.ds(h * HD, HD)]

    def a_remote(s, t, h):
        return rcopy(a_src(s, h), a_at(g, c, h), at_s.at[s, t, h], at_r.at[g, h], owner(s, t))

    def a_local(s, h):
        return pltpu.make_async_copy(a_src(s, h), a_at(g, c, h), at_r.at[g, h])

    def finish(s):
        u = chunk_of(s)
        l_ref[u, 0:1, :] = jnp.sum(l_ref[u], axis=0, keepdims=True)

        def merge(xs, s=s, u=u):
            rcopy(osend.at[u], orecv.at[xs, s], os_s.at[u, 0], os_r.at[xs, s, 0], sib).wait_recv()
            rcopy(ssend.at[u], srecv.at[xs, s], os_s.at[u, 1], os_r.at[xs, s, 1], sib).wait_recv()
            m_old = m_ref[u, 0:1, :]
            m_in = srecv[xs, s, 0:1, :]
            m_new = jnp.maximum(m_old, m_in)
            a_old = jnp.exp2(m_old - m_new)
            a_in = jnp.exp2(m_in - m_new)
            m_ref[u, 0:1, :] = m_new
            l_ref[u, 0:1, :] = l_ref[u, 0:1, :] * a_old + srecv[xs, s, 4:5, :] * a_in
            acc[u] = acc[u] * a_old + orecv[xs, s].astype(F32) * a_in

        for xs in range(NX):
            there = xs < x if xs > 0 else jnp.logical_and(x > 0, x < NX - 1)
            pl.when(there)(functools.partial(merge, xs))
        for h in range(2):
            o = acc[u, :, hs(h)] * (1.0 / l_ref[u, 0:1, hs(h)])
            attsend[s, :, h * HD:(h + 1) * HD] = o.astype(BF).T
            for t in range(2):
                here = owned(s, t)

                @pl.when(here)
                def _():
                    a_local(s, h).start()

                @pl.when(jnp.logical_not(here))
                def _():
                    a_remote(s, t, h).start()

    def w_on(j):
        w1_in(j).wait_recv()
        w2(j).start()

    n = top - lo + 1
    far = top - hi

    def far_end(go, *args):
        pl.when(at_end)(functools.partial(go, *args))

    def when(cond, *acts):
        @pl.when(cond)
        def _():
            for act in acts:
                act()

    def each(go, rs, e=0):
        return lambda: [go(r, e) for r in rs]

    def unit_loop(count, at, blocks, before, after):
        @pl.when(count > 0)
        def _():
            for h in range(2):
                score(blocks(0), at(0), h)

        def one(i, _):
            u = at(i)
            nxt = jnp.minimum(i + 1, count - 1)
            un = at(nxt)
            before(i, u, un)
            for h in range(2):
                absorb(blocks(i), u, blocks(nxt), un, h)
            after(i, u)
            return 0

        lax.fori_loop(0, count, one, 0)

    def ring(e, _):
        base = 2 * e
        own = e == 0
        extra = jnp.logical_and(e == 1, at_end)
        when(own, arrive_two, lambda: w_on(0), each(sib_arrive, (3,)))
        when(extra, each(arrive, (1, 2), 1), each(sib_arrive, (0, 3), 1))

        def at_first(i):
            return jnp.where(own, lo + i, hi - i)

        def before_first(i, u, un):
            when(jnp.logical_and(own, i == n // 2), each(arrive, (1, 2)),
                 lambda: far_end(launch_one, 1), lambda: w_on(1))
            when(jnp.logical_and(own, jnp.logical_and(un > u, un > hi)), lambda: q_wait(un))

        few = jnp.where(at_end, 2, 0)
        unit_loop(jnp.where(own, n, few), at_first,
                  lambda i: [(base + b, rel[r]) for r in (0, 3) for b in range(2)], before_first, lambda i, u: None)

        def rest(t, _):
            first = jnp.logical_and(own, t == 0)
            last = jnp.logical_and(own, t == 1)
            ends = jnp.logical_and(own, t == 2)
            when(first, each(sib_arrive, (1, 2, 4)), lambda: far_end(arrive_two, 1), lambda: w_on(2))
            when(jnp.logical_and(last, far == 0), each(arrive, (5, 6, 7)))
            when(last, each(sib_arrive, (5, 6, 7)), lambda: pl.when(jnp.logical_not(at_end))(lambda: w_on(3)))
            when(jnp.logical_and(extra, t == 0), each(sib_arrive, (1, 2, 4), 1))
            when(jnp.logical_and(extra, t == 1), each(arrive, (5, 6, 7), 1), each(sib_arrive, (5, 6, 7), 1))

            def at(i):
                return jnp.where(first, hi + 1 + i, jnp.where(last, top - i, jnp.where(ends, hi - i // 2, hi - i)))

            def before(i, u, un):
                when(jnp.logical_and(first, i == far // 2), each(arrive, (5, 6, 7)))
                when(jnp.logical_and(ends, jnp.logical_and(at_end, i == 2)), lambda: w_on(3))

            def after(i, u):
                @pl.when(last)
                def _():
                    osend[u] = acc[u].astype(BF)
                    lsum = jnp.sum(l_ref[u], axis=0, keepdims=True)
                    ssend[u] = jnp.concatenate(
                        [jnp.broadcast_to(m_ref[u, 0:1, :], (4, 2 * ROWS)),
                         jnp.broadcast_to(lsum, (4, 2 * ROWS))], axis=0)
                    o_send(u).start()
                    st_send(u).start()

                complete = jnp.where(at_end, jnp.logical_and(jnp.logical_and(extra, t == 1), i == 0),
                                     jnp.logical_and(ends, i == 1))
                when(complete, lambda: finish(1))

            def blocks(i):
                early = jnp.logical_or(t == 0, jnp.logical_and(t == 2, i % 2 == 0))
                zs = [jnp.where(early, rel[a], rel[b]) for a, b in ((1, 5), (2, 6), (4, 7))]
                return [(base + b, zz) for zz in zs for b in range(2)]

            unit_loop(jnp.where(t == 2, jnp.where(own, 4, 0), jnp.where(own, far, few)), at, blocks, before, after)
            return 0

        lax.fori_loop(0, 3, rest, 0)
        return 0

    lax.fori_loop(0, 2, ring, 0)
    finish(0)

    def a_sib(gg, h):
        return rcopy(a_at(gg, c, h), a_at(gg, c, h), as_s.at[gg, h], as_r.at[gg, h], sib)

    for h in range(2):
        for gg in range(4):
            pltpu.make_async_copy(a_src(0, h), a_at(gg, c, h), at_r.at[gg, h]).wait()
            a_sib(gg, h).start()
    w3.wait_recv()
    wown.wait()
    for j in range(WCH):
        rcopy(wbuf.at[yrow, pl.ds(j * WP, WP), :], wbuf.at[yrow, pl.ds(j * WP, WP), :],
              w2_s.at[j], w2_r.at[j], sib).wait_recv()

    KH = 2 * HD

    def project(core, j):
        rows = jnp.concatenate([att[i, core] for i in range(4)], axis=1)
        wcol = jnp.concatenate(
            [wbuf[i, pl.ds(pl.multiple_of(core * KH, KH), KH), j * 256:(j + 1) * 256] for i in range(4)], axis=0)
        return jnp.dot(rows, wcol, preferred_element_type=F32)

    for j in range(DC // 256):
        part[:, j * 256:(j + 1) * 256] = project(c, j)
    for h in range(2):
        for gg in range(4):
            rcopy(a_at(gg, 1 - c, h), a_at(gg, 1 - c, h), as_s.at[gg, h], as_r.at[gg, h], sib).wait_recv()
    for j in range(DC // 256):
        cs = slice(j * 256, (j + 1) * 256)
        o_ref[:, cs] = (part[:, cs] + project(1 - c, j)).astype(BF)

    @pl.when(x == 0)
    def _():
        kcp2.wait_send()
        vcp2.wait_send()

    q_each(lambda cp: cp.wait_send(), None)

    @pl.when(c != yl)
    def _():
        for j in range(WCH):
            for d in range(2):
                w1(j, d).wait_send()
    for j in range(WCH):
        w2(j).wait_send()
    w3.wait_send()
    drained(0)

    @pl.when(at_end)
    def _():
        drained(1)

    def sent(u, _):
        o_send(u).wait_send()
        st_send(u).wait_send()
        return 0

    lax.fori_loop(hi + 1, top + 1, sent, 0)
    for s in range(2):
        for t in range(2):
            @pl.when(jnp.logical_not(owned(s, t)))
            def _():
                for h in range(2):
                    a_remote(s, t, h).wait_send()
    for gg in range(4):
        for h in range(2):
            a_sib(gg, h).wait_send()


def per_device(query, keys, values, out_weight):
    rows = query.shape[0]
    d_model = out_weight.shape[1]
    dma = pltpu.SemaphoreType.DMA
    vm = pl.BlockSpec(memory_space=pltpu.VMEM)
    hbm = pl.BlockSpec(memory_space=pltpu.HBM)
    R2 = 2 * ROWS
    return pl.pallas_call(
        kernel,
        out_shape=jax.ShapeDtypeStruct((rows, d_model // 4), BF),
        in_specs=[hbm, hbm, hbm, hbm],
        out_specs=vm,
        scratch_shapes=[
            pltpu.VMEM((ROWS, HD), BF),
            pltpu.VMEM((ROWS, HD), BF),
            pltpu.VMEM((4, NZ, R2, HD), BF),
            pltpu.VMEM((NU, ROWS, 2 * HD), BF),
            pltpu.VMEM((6 * ROWS, R2), F32),
            pltpu.VMEM((8, R2), F32),
            pltpu.VMEM((NU, HD, R2), F32),
            pltpu.VMEM((NU, 8, R2), F32),
            pltpu.VMEM((NU, 8, R2), F32),
            pltpu.VMEM((NU, HD, R2), BF),
            pltpu.VMEM((NU, 8, R2), F32),
            pltpu.VMEM((NX, 2, HD, R2), BF),
            pltpu.VMEM((NX, 2, 8, R2), F32),
            pltpu.VMEM((2, ROWS, 2 * HD), BF),
            pltpu.VMEM((4, 2, ROWS, 2 * HD), BF),
            pltpu.VMEM((4, out_weight.shape[0], d_model // 4), BF),
            pltpu.VMEM((rows, d_model // 4), F32),
            dma((4,)), dma((4,)),
            dma((NX, 2)), dma((NU,)),
            dma((2, NZ, 2)), dma((2, NZ, 2)),
            dma((2, 8)), dma((2, 8)),
            dma((WCH, 2)), dma((WCH,)), dma((WCH,)), dma((WCH,)), dma, dma, dma, dma,
            dma((NU, 2)), dma((NX, 2, 2)),
            dma((2, 2, 2)), dma((4, 2)), dma((4, 2)), dma((4, 2)),
        ],
        compiler_params=pltpu.CompilerParams(
            collective_id=0, has_side_effects=True, vmem_limit_bytes=48 * 1024 * 1024
        ),
    )(query, keys, values, out_weight)


def solution(mesh):
    return jax.shard_map(
        per_device,
        mesh=mesh,
        in_specs=(P("ctx", "head"), P("ctx", "head"), P("ctx", "head"), P("head", None)),
        out_specs=P("ctx", "head"),
        check_vma=False,
    )
```

```python
import functools
import math

import jax
import jax.numpy as jnp
from jax import lax
from jax.experimental import pallas as pl
from jax.experimental.pallas import tpu as pltpu
from jax.sharding import PartitionSpec as P

HD = 128
ROWS = 256
NX, NZ = 4, 8
NU = 2 * NX
LOG2E = math.log2(math.e)
FLOOR = -1e30
PEN = 1e32
WCH = 4
MESH = pl.DeviceIdType.MESH
MIRROR = (0, 2, 1, 4, 3)
BF = jnp.bfloat16
F32 = jnp.float32


def low_of(x):
    return 2 * x


def column_of(u):
    return u // 2


def slot_of(u):
    return u % 2


def dev(x, yl, z, yh, c):
    return {"ctx": (x * 2 + yl) * NZ + z, "head": yh * 2 + c}


def kernel(
    q_ref, k_ref, v_ref, w_ref, o_ref,
    vraw, vst, kvbuf, qbuf, s_ref, mx_ref, acc, m_ref, l_ref,
    osend, ssend, orecv, srecv, attsend, att, wbuf, part,
    sw_s, sw_r, qs_s, qs_r, z_s, z_r, sib_s, sib_r,
    w1_s, w1_r, w2_s, w2_r, w3_s, w3_r, wl, vl,
    os_s, os_r, at_s, at_r, as_s, as_r,
):
    ctx = lax.axis_index("ctx")
    head = lax.axis_index("head")
    x = ctx // (2 * NZ)
    yl = (ctx // NZ) % 2
    z = ctx % NZ
    yh = head // 2
    c = head % 2
    scale = LOG2E / math.sqrt(HD)
    D = functools.partial(dev)
    zp, zm = (z + 1) % NZ, (z + NZ - 1) % NZ

    vcopy = pltpu.make_async_copy(v_ref, vraw, vl)
    vcopy.start()
    barrier = pltpu.get_barrier_semaphore()
    partners = []
    for i in range(1, 4 * NX):
        partners.append(D((x + i // 4) % NX, (yl + (i // 2) % 2) % 2, z, yh, (c + i % 2) % 2))
    for i in range(2):
        partners.append(D(x, i, z, 1 - yh, c))
    partners.append(D(x, 1 - yl, z, 1 - yh, 1 - c))
    rel = [z, zm, zp, (z + NZ - 2) % NZ, (z + 2) % NZ, (z + NZ - 3) % NZ, (z + 3) % NZ,
           (z + NZ - 4) % NZ]
    partners += [D(x, yl, rel[r], yh, c) for r in (1, 2, 3, 4)]
    for p in partners:
        pl.semaphore_signal(barrier, inc=1, device_id=p, device_id_type=MESH)
    vcopy.wait()
    vst[0:HD, :] = vraw[0:HD, :].T
    vst[HD:ROWS, :] = vraw[HD:ROWS, :].T
    pl.semaphore_wait(barrier, len(partners))

    def rcopy(src, dst, ss, rs, to):
        return pltpu.make_async_remote_copy(
            src_ref=src, dst_ref=dst, send_sem=ss, recv_sem=rs, device_id=to, device_id_type=MESH
        )

    sib = D(x, yl, z, yh, 1 - c)
    lo = low_of(x)
    hi = lo + 1
    top = jnp.where(x == 0, NU - 3, NU - 1)
    at_end = x == NX - 1
    mine = 2 * x + yl

    col, slo = column_of(mine), slot_of(mine)
    home = D(col, c, z, yh, slo)
    stays = jnp.logical_and(jnp.logical_and(col == x, c == yl), slo == c)

    def kv_half(slot, zz, half):
        return kvbuf.at[slot, zz, pl.ds(half * ROWS, ROWS), :]

    kcp = rcopy(k_ref, kv_half(slo, z, 0), sw_s.at[0], sw_r.at[0], home)
    vcp = rcopy(vst, kv_half(slo, z, 1), sw_s.at[1], sw_r.at[1], home)
    klc = pltpu.make_async_copy(k_ref, kv_half(slo, z, 0), sw_r.at[0])
    vlc = pltpu.make_async_copy(vst, kv_half(slo, z, 1), sw_r.at[1])

    home2 = D(NX - 1, c, z, yh, slo)
    kcp2 = rcopy(k_ref, kv_half(2 + slo, z, 0), sw_s.at[2], sw_r.at[2], home2)
    vcp2 = rcopy(vst, kv_half(2 + slo, z, 1), sw_s.at[3], sw_r.at[3], home2)

    @pl.when(jnp.logical_not(stays))
    def _():
        kcp.start()
        vcp.start()

    @pl.when(x == 0)
    def _():
        kcp2.start()
        vcp2.start()

    @pl.when(stays)
    def _():
        klc.start()
        vlc.start()

    def q_src(d):
        return q_ref.at[:, pl.ds(d * 2 * HD, 2 * HD)]

    def q_each(remote, local, which=range(NX)):
        for i in which:
            xt = (col + i) % NX
            for d in range(2):
                want = jnp.logical_and(low_of(xt) <= mine, jnp.logical_or(xt > 0, mine < NU - 2))
                here = jnp.logical_and(jnp.logical_and(xt == x, c == yl), c == d)

                @pl.when(jnp.logical_and(want, jnp.logical_not(here)))
                def _(i=i, d=d, xt=xt):
                    remote(rcopy(q_src(d), qbuf.at[mine], qs_s.at[i, d], qs_r.at[mine], D(xt, c, z, yh, d)))

                if local is not None:
                    @pl.when(jnp.logical_and(want, here))
                    def _(d=d):
                        local(pltpu.make_async_copy(q_src(d), qbuf.at[mine], qs_r.at[mine]))


    DC = o_ref.shape[1]
    WR = w_ref.shape[0]
    WP = WR // WCH
    gw = yh * 2 + c
    xrow = (1 - yh) * 2 + yl
    yrow = (1 - yh) * 2 + (1 - yl)

    def w1(j, d):
        return rcopy(
            w_ref.at[pl.ds(j * WP, WP), pl.ds(((1 - yh) * 2 + d) * DC, DC)],
            wbuf.at[gw, pl.ds(j * WP, WP), :],
            w1_s.at[j, d], w1_r.at[j], D(x, 1 - yl, z, 1 - yh, d),
        )

    def w1_in(j):
        return rcopy(
            wbuf.at[xrow, pl.ds(j * WP, WP), :], wbuf.at[xrow, pl.ds(j * WP, WP), :],
            w2_s.at[j], w1_r.at[j], D(x, 1 - yl, z, yh, c),
        )

    def w2(j):
        return rcopy(
            wbuf.at[xrow, pl.ds(j * WP, WP), :], wbuf.at[xrow, pl.ds(j * WP, WP), :],
            w2_s.at[j], w2_r.at[j], D(x, 1 - yl, z, yh, c),
        )

    w3 = rcopy(
        w_ref.at[:, pl.ds((yh * 2 + 1 - c) * DC, DC)], wbuf.at[gw], w3_s, w3_r, sib
    )
    wown = pltpu.make_async_copy(w_ref.at[:, pl.ds(gw * DC, DC)], wbuf.at[gw], wl)

    def blk(slot, zz):
        return kvbuf.at[slot, zz]

    def zto(r):
        return D(x, yl, rel[r], yh, c)

    def half_of(slot, zz, h):
        return kvbuf.at[slot, zz, pl.ds(h * ROWS, ROWS), :]

    def own_to(r, h, e=0):
        src = half_of(2 * e + c, z, h)
        return rcopy(src, src, z_s.at[e, r, h], z_r.at[e, MIRROR[r], h], zto(r))

    def pass_on(r, h, e=0):
        src = half_of(2 * e + c, rel[r], h)
        return rcopy(src, src, z_s.at[e, r + 2, h], z_r.at[e, r + 2, h], zto(5 - r))

    def pass_half(r, e=0):
        src = half_of(2 * e + c, rel[r], r - 3)
        return rcopy(src, src, z_s.at[e, 7, r - 3], z_r.at[e, 7, r - 3], zto(7 - r))

    def tosib(r, e=0):
        src = blk(2 * e + c, rel[r])
        return rcopy(src, src, sib_s.at[e, r], sib_r.at[e, r], sib)

    def landed(r, h, e):
        src = half_of(2 * e + c, rel[r], h)
        rcopy(src, src, z_s.at[e, 0, 0], z_r.at[e, r, h], sib).wait_recv()

    def arrive(r, e=0):
        for h in range(2):
            landed(r, h, e)
        tosib(r, e).start()

    def arrive_two(e=0):
        for h in range(2):
            for r in (3, 4):
                landed(r, h, e)
                pass_on(r, h, e).start()
                if h == r - 3:
                    pass_half(r, e).start()
        for r in (3, 4):
            tosib(r, e).start()

    def sib_arrive(r, e=0):
        src = blk(2 * e + 1 - c, rel[r])
        rcopy(src, src, sib_s.at[e, r], sib_r.at[e, r], sib).wait_recv()

    def launch_two(e):
        for h in range(2):
            src = half_of(2 * e + c, z, h)
            pltpu.make_async_copy(src, src, sw_r.at[2 * e + h]).wait()
            for r in (3, 4):
                own_to(r, h, e).start()
        tosib(0, e).start()

    def launch_one(e):
        for h in range(2):
            for r in (3, 4):
                own_to(r, h, e).wait_send()
            for r in (1, 2):
                own_to(r, h, e).start()

    def drained(e):
        for h in range(2):
            for r in (1, 2):
                own_to(r, h, e).wait_send()
            for r in (3, 4):
                pass_on(r, h, e).wait_send()
        for r in (3, 4):
            pass_half(r, e).wait_send()
        for r in range(8):
            tosib(r, e).wait_send()

    @pl.when(c != yl)
    def _():
        for j in range(WCH):
            for d in range(2):
                w1(j, d).start()

    m_ref[...] = jnp.full_like(m_ref, FLOOR)
    l_ref[...] = jnp.zeros_like(l_ref)
    acc[...] = jnp.zeros_like(acc)
    @pl.when(jnp.logical_not(stays))
    def _():
        kcp.wait_send()
        vcp.wait_send()

    q_each(lambda cp: cp.start(), lambda cp: cp.start(), (0,))

    launch_two(0)
    q_each(lambda cp: cp.start(), lambda cp: cp.start(), (1, 2, 3))

    def q_wait(u):
        pltpu.make_async_copy(qbuf.at[u], qbuf.at[u], qs_r.at[u]).wait()

    q_wait(lo)
    q_wait(hi)
    w3.start()
    wown.start()

    def hs(h):
        return slice(h * ROWS, (h + 1) * ROWS)

    def qk(slot, zz, u, h):
        return lax.dot_general(
            kvbuf[slot, zz, 0:ROWS, :], qbuf[u, :, h * HD:(h + 1) * HD],
            (((1,), (1,)), ((), ())), preferred_element_type=F32,
        )

    def vt(slot, zz):
        return jnp.concatenate(
            [kvbuf[slot, zz, ROWS:ROWS + HD, :], kvbuf[slot, zz, ROWS + HD:2 * ROWS, :]], axis=1
        )

    def pv(slot, zz, p):
        return lax.dot_general(
            vt(slot, zz), p.astype(BF), (((1,), (0,)), ((), ())), preferred_element_type=F32
        )

    def fold(a, op):
        return op(a.reshape(a.shape[0] // 8, 8, a.shape[1]), axis=0)

    def diagonal(slot, u):
        key_i = lax.broadcasted_iota(jnp.int32, (ROWS, ROWS), 0)
        qry_i = lax.broadcasted_iota(jnp.int32, (ROWS, ROWS), 1)
        allowed = key_i <= qry_i
        for h in range(2):
            s = jnp.where(allowed, qk(slot, z, u, h) * scale, -PEN)
            m = jnp.max(s, axis=0, keepdims=True)
            p = jnp.exp2(s - m)
            m_ref[u, 0:1, hs(h)] = m
            l_ref[u, :, hs(h)] = fold(p, jnp.sum)
            acc[u, :, hs(h)] = pv(slot, z, p)

    def chunk(slot):
        return jnp.where(slot < 2, lo + slot, slot - 2)

    def pen(slot, zz, u):
        kid = chunk(slot) * NZ + zz
        return jnp.where(kid < u * NZ + z, 0.0, PEN).astype(F32)

    def score(blocks, u, h):
        mx = None
        for b, (slot, zz) in enumerate(blocks):
            s = qk(slot, zz, u, h)
            s_ref[b * ROWS:(b + 1) * ROWS, hs(h)] = s
            top = fold(s, jnp.max) - pen(slot, zz, u)
            mx = top if mx is None else jnp.maximum(mx, top)
        mx_ref[:, hs(h)] = mx

    def absorb(blocks, u, blocks_next, un, h):
        m_old = m_ref[u, 0:1, hs(h)]
        m_new = jnp.maximum(m_old, jnp.max(mx_ref[:, hs(h)], axis=0, keepdims=True) * scale)
        alpha = jnp.exp2(m_old - m_new)
        m_ref[u, 0:1, hs(h)] = m_new
        l8, out = None, None
        for b, (slot, zz) in enumerate(blocks):
            p = jnp.exp2(s_ref[b * ROWS:(b + 1) * ROWS, hs(h)] * scale - (m_new + pen(slot, zz, u)))
            p8 = fold(p, jnp.sum)
            l8 = p8 if l8 is None else l8 + p8
            d = pv(slot, zz, p)
            out = d if out is None else out + d
        score(blocks_next, un, h)
        l_ref[u, :, hs(h)] = l_ref[u, :, hs(h)] * alpha + l8
        acc[u, :, hs(h)] = acc[u, :, hs(h)] * alpha + out

    diagonal(c, chunk(c))
    launch_one(0)
    sib_arrive(0)
    diagonal(1 - c, chunk(1 - c))

    @pl.when(at_end)
    def _():
        launch_two(1)

    def o_send(u):
        return rcopy(osend.at[u], orecv.at[x, slot_of(u)], os_s.at[u, 0],
                     os_r.at[x, slot_of(u), 0], D(column_of(u), yl, z, yh, c))

    def st_send(u):
        return rcopy(ssend.at[u], srecv.at[x, slot_of(u)], os_s.at[u, 1],
                     os_r.at[x, slot_of(u), 1], D(column_of(u), yl, z, yh, c))

    g = yh * 2 + yl

    def chunk_of(s):
        return lo if s == 0 else hi

    def owner(s, t):
        u = chunk_of(s)
        return D(u // 2, u % 2, z, t, c)

    def owned(s, t):
        u = chunk_of(s)
        return jnp.logical_and(u == mine, yh == t)

    def a_src(s, h):
        return attsend.at[s, :, pl.ds(h * HD, HD)]

    def a_at(gg, core, h):
        return att.at[gg, core, :, pl.ds(h * HD, HD)]

    def a_remote(s, t, h):
        return rcopy(a_src(s, h), a_at(g, c, h), at_s.at[s, t, h], at_r.at[g, h], owner(s, t))

    def a_local(s, h):
        return pltpu.make_async_copy(a_src(s, h), a_at(g, c, h), at_r.at[g, h])

    def finish(s):
        u = chunk_of(s)
        l_ref[u, 0:1, :] = jnp.sum(l_ref[u], axis=0, keepdims=True)

        def merge(xs, s=s, u=u):
            rcopy(osend.at[u], orecv.at[xs, s], os_s.at[u, 0], os_r.at[xs, s, 0], sib).wait_recv()
            rcopy(ssend.at[u], srecv.at[xs, s], os_s.at[u, 1], os_r.at[xs, s, 1], sib).wait_recv()
            m_old = m_ref[u, 0:1, :]
            m_in = srecv[xs, s, 0:1, :]
            m_new = jnp.maximum(m_old, m_in)
            a_old = jnp.exp2(m_old - m_new)
            a_in = jnp.exp2(m_in - m_new)
            m_ref[u, 0:1, :] = m_new
            l_ref[u, 0:1, :] = l_ref[u, 0:1, :] * a_old + srecv[xs, s, 4:5, :] * a_in
            acc[u] = acc[u] * a_old + orecv[xs, s].astype(F32) * a_in

        for xs in range(NX):
            there = xs < x if xs > 0 else jnp.logical_and(x > 0, x < NX - 1)
            pl.when(there)(functools.partial(merge, xs))
        for h in range(2):
            o = acc[u, :, hs(h)] * (1.0 / l_ref[u, 0:1, hs(h)])
            attsend[s, :, h * HD:(h + 1) * HD] = o.astype(BF).T
            for t in range(2):
                here = owned(s, t)

                @pl.when(here)
                def _():
                    a_local(s, h).start()

                @pl.when(jnp.logical_not(here))
                def _():
                    a_remote(s, t, h).start()

    def w_on(j):
        w1_in(j).wait_recv()
        w2(j).start()

    n = top - lo + 1
    far = top - hi

    def far_end(go, *args):
        pl.when(at_end)(functools.partial(go, *args))

    def when(cond, *acts):
        @pl.when(cond)
        def _():
            for act in acts:
                act()

    def each(go, rs, e=0):
        return lambda: [go(r, e) for r in rs]

    def unit_loop(count, at, blocks, before, after):
        @pl.when(count > 0)
        def _():
            for h in range(2):
                score(blocks(0), at(0), h)

        def one(i, _):
            u = at(i)
            nxt = jnp.minimum(i + 1, count - 1)
            un = at(nxt)
            before(i, u, un)
            for h in range(2):
                absorb(blocks(i), u, blocks(nxt), un, h)
            after(i, u)
            return 0

        lax.fori_loop(0, count, one, 0)

    def ring(e, _):
        base = 2 * e
        own = e == 0
        extra = jnp.logical_and(e == 1, at_end)
        when(own, arrive_two, lambda: w_on(0), each(sib_arrive, (3,)))
        when(extra, each(arrive, (1, 2), 1), each(sib_arrive, (0, 3), 1))

        def at_first(i):
            return jnp.where(own, lo + i, hi - i)

        def before_first(i, u, un):
            when(jnp.logical_and(own, i == n // 2), each(arrive, (1, 2)),
                 lambda: far_end(launch_one, 1), lambda: w_on(1))
            when(jnp.logical_and(own, jnp.logical_and(un > u, un > hi)), lambda: q_wait(un))

        few = jnp.where(at_end, 2, 0)
        unit_loop(jnp.where(own, n, few), at_first,
                  lambda i: [(base + b, rel[r]) for r in (0, 3) for b in range(2)], before_first, lambda i, u: None)

        def rest(t, _):
            first = jnp.logical_and(own, t == 0)
            last = jnp.logical_and(own, t == 1)
            ends = jnp.logical_and(own, t == 2)
            when(first, each(sib_arrive, (1, 2, 4)), lambda: far_end(arrive_two, 1), lambda: w_on(2))
            when(jnp.logical_and(last, far == 0), each(arrive, (5, 6, 7)))
            when(last, each(sib_arrive, (5, 6, 7)), lambda: pl.when(jnp.logical_not(at_end))(lambda: w_on(3)))
            when(jnp.logical_and(extra, t == 0), each(sib_arrive, (1, 2, 4), 1))
            when(jnp.logical_and(extra, t == 1), each(arrive, (5, 6, 7), 1), each(sib_arrive, (5, 6, 7), 1))

            def at(i):
                return jnp.where(first, hi + 1 + i, jnp.where(last, top - i, jnp.where(ends, hi - i // 2, hi - i)))

            def before(i, u, un):
                when(jnp.logical_and(first, i == far // 2), each(arrive, (5, 6, 7)))
                when(jnp.logical_and(ends, jnp.logical_and(at_end, i == 2)), lambda: w_on(3))

            def after(i, u):
                @pl.when(last)
                def _():
                    osend[u] = acc[u].astype(BF)
                    lsum = jnp.sum(l_ref[u], axis=0, keepdims=True)
                    ssend[u] = jnp.concatenate(
                        [jnp.broadcast_to(m_ref[u, 0:1, :], (4, 2 * ROWS)),
                         jnp.broadcast_to(lsum, (4, 2 * ROWS))], axis=0)
                    o_send(u).start()
                    st_send(u).start()

                complete = jnp.where(at_end, jnp.logical_and(jnp.logical_and(extra, t == 1), i == 0),
                                     jnp.logical_and(ends, i == 1))
                when(complete, lambda: finish(1))

            def blocks(i):
                early = jnp.logical_or(t == 0, jnp.logical_and(t == 2, i % 2 == 0))
                zs = [jnp.where(early, rel[a], rel[b]) for a, b in ((1, 5), (2, 6), (4, 7))]
                return [(base + b, zz) for zz in zs for b in range(2)]

            unit_loop(jnp.where(t == 2, jnp.where(own, 4, 0), jnp.where(own, far, few)), at, blocks, before, after)
            return 0

        lax.fori_loop(0, 3, rest, 0)
        return 0

    lax.fori_loop(0, 2, ring, 0)
    finish(0)

    def a_sib(gg, h):
        return rcopy(a_at(gg, c, h), a_at(gg, c, h), as_s.at[gg, h], as_r.at[gg, h], sib)

    for h in range(2):
        for away in (0, 1, 3, 2):
            gg = (g + away) % 4
            pltpu.make_async_copy(a_src(0, h), a_at(gg, c, h), at_r.at[gg, h]).wait()
            a_sib(gg, h).start()
    w3.wait_recv()
    wown.wait()
    for j in range(WCH):
        rcopy(wbuf.at[yrow, pl.ds(j * WP, WP), :], wbuf.at[yrow, pl.ds(j * WP, WP), :],
              w2_s.at[j], w2_r.at[j], sib).wait_recv()

    KH = 2 * HD

    def project(core, j):
        rows = jnp.concatenate([att[i, core] for i in range(4)], axis=1)
        wcol = jnp.concatenate(
            [wbuf[i, pl.ds(pl.multiple_of(core * KH, KH), KH), j * 256:(j + 1) * 256] for i in range(4)], axis=0)
        return jnp.dot(rows, wcol, preferred_element_type=F32)

    for j in range(DC // 256):
        part[:, j * 256:(j + 1) * 256] = project(c, j)
    for h in range(2):
        for gg in range(4):
            rcopy(a_at(gg, 1 - c, h), a_at(gg, 1 - c, h), as_s.at[gg, h], as_r.at[gg, h], sib).wait_recv()
    for j in range(DC // 256):
        cs = slice(j * 256, (j + 1) * 256)
        o_ref[:, cs] = (part[:, cs] + project(1 - c, j)).astype(BF)

    @pl.when(x == 0)
    def _():
        kcp2.wait_send()
        vcp2.wait_send()

    q_each(lambda cp: cp.wait_send(), None)

    @pl.when(c != yl)
    def _():
        for j in range(WCH):
            for d in range(2):
                w1(j, d).wait_send()
    for j in range(WCH):
        w2(j).wait_send()
    w3.wait_send()
    drained(0)

    @pl.when(at_end)
    def _():
        drained(1)

    def sent(u, _):
        o_send(u).wait_send()
        st_send(u).wait_send()
        return 0

    lax.fori_loop(hi + 1, top + 1, sent, 0)
    for s in range(2):
        for t in range(2):
            @pl.when(jnp.logical_not(owned(s, t)))
            def _():
                for h in range(2):
                    a_remote(s, t, h).wait_send()
    for gg in range(4):
        for h in range(2):
            a_sib(gg, h).wait_send()


def per_device(query, keys, values, out_weight):
    rows = query.shape[0]
    d_model = out_weight.shape[1]
    dma = pltpu.SemaphoreType.DMA
    vm = pl.BlockSpec(memory_space=pltpu.VMEM)
    hbm = pl.BlockSpec(memory_space=pltpu.HBM)
    R2 = 2 * ROWS
    return pl.pallas_call(
        kernel,
        out_shape=jax.ShapeDtypeStruct((rows, d_model // 4), BF),
        in_specs=[hbm, hbm, hbm, hbm],
        out_specs=vm,
        scratch_shapes=[
            pltpu.VMEM((ROWS, HD), BF),
            pltpu.VMEM((ROWS, HD), BF),
            pltpu.VMEM((4, NZ, R2, HD), BF),
            pltpu.VMEM((NU, ROWS, 2 * HD), BF),
            pltpu.VMEM((6 * ROWS, R2), F32),
            pltpu.VMEM((8, R2), F32),
            pltpu.VMEM((NU, HD, R2), F32),
            pltpu.VMEM((NU, 8, R2), F32),
            pltpu.VMEM((NU, 8, R2), F32),
            pltpu.VMEM((NU, HD, R2), BF),
            pltpu.VMEM((NU, 8, R2), F32),
            pltpu.VMEM((NX, 2, HD, R2), BF),
            pltpu.VMEM((NX, 2, 8, R2), F32),
            pltpu.VMEM((2, ROWS, 2 * HD), BF),
            pltpu.VMEM((4, 2, ROWS, 2 * HD), BF),
            pltpu.VMEM((4, out_weight.shape[0], d_model // 4), BF),
            pltpu.VMEM((rows, d_model // 4), F32),
            dma((4,)), dma((4,)),
            dma((NX, 2)), dma((NU,)),
            dma((2, NZ, 2)), dma((2, NZ, 2)),
            dma((2, 8)), dma((2, 8)),
            dma((WCH, 2)), dma((WCH,)), dma((WCH,)), dma((WCH,)), dma, dma, dma, dma,
            dma((NU, 2)), dma((NX, 2, 2)),
            dma((2, 2, 2)), dma((4, 2)), dma((4, 2)), dma((4, 2)),
        ],
        compiler_params=pltpu.CompilerParams(
            collective_id=0, has_side_effects=True, vmem_limit_bytes=48 * 1024 * 1024
        ),
    )(query, keys, values, out_weight)


def solution(mesh):
    return jax.shard_map(
        per_device,
        mesh=mesh,
        in_specs=(P("ctx", "head"), P("ctx", "head"), P("ctx", "head"), P("head", None)),
        out_specs=P("ctx", "head"),
        check_vma=False,
    )
```
